32 devices in a mesh: prow: 4 (over z), pcol: 8 (over y, x, core).
Axes of the slice: x: 2, y: 2, z: 4, core: 2. Of those that a mesh axis runs over, the one named last changes fastest.
Arguments:
- window_rhs: float32 [64, 4096], P(None, 'prow'), may hold values from -6 to 6
- past_solution: float32 [64, 16384], P(None, 'pcol'), may hold values from -6 to 6
- past_panel: float32 [4096, 16384], P('prow', 'pcol'), may hold values from -0.046875 to 0.046875
- window_panel: float32 [4, 1024, 8, 1024], P('prow', None, 'pcol'), may hold values from -0.09375 to 0.09375
- diag_inverse: float32 [4, 1024, 1024], P('prow'), may hold values from -1 to 1.5, as said below
- tile_list: int32 [32, 2], P(('prow', 'pcol')), may hold values from 0 to 31
- neighbor_list: int32 [32, 2, 8], P(('prow', 'pcol')), may hold values from 0 to 31
- force_constants: float32 [32, 2, 8, 128, 128], P(('prow', 'pcol')), may hold values from -0.1875 to 0.1875
Outputs:
- solution: float32 [64, 4096], P(None, 'prow')
- residual_forces: float32 [32, 2, 64, 128], P(('prow', 'pcol'))
The draws below stay inside these ranges and needn't reach their ends.
Inputs may be any that keep to these rules, and one draw needn't show every extreme that they name: `diag_inverse`: each block is lower triangular, with diagonal entries from 0.6 to 1.4.
All inputs are finite; a program needn't handle non-finite values.
Results may differ from the reference program's by a relative error of at most 0.00011.
Values sent between devices are 32-bit elements; how exact they have to be, the bound alone decides.
A program may use at most 128 MiB of HBM per device.

```python
import jax
import jax.numpy as jnp
from jax import lax

NB = 1024
NRHS = 64
TILE = 128
NNB = 8
TPD = 2
WB = 4
COLS = 8
PAST = 16
TILES = 32
DEVICES = 32


def draw_diag_inverse(key, part):
    first, second = jax.random.split(key)
    lower = jax.random.normal(first, (WB, NB, NB), jnp.float32) * (0.6 / NB ** 0.5)
    lower = jnp.clip(lower, -0.9, 0.9)
    rows = jnp.arange(NB)[:, None]
    cols = jnp.arange(NB)[None, :]
    below = (rows > cols).astype(jnp.float32)
    same = (rows == cols).astype(jnp.float32)
    diagonal = jax.random.uniform(second, (WB, NB), jnp.float32, 0.6, 1.4)
    return lower * below[None] + diagonal[:, :, None] * same[None]


def touch_ends(array, key, smallest, high):
    dims = array.shape
    spot = [jax.random.randint(jax.random.fold_in(key, axis), (), 0, dims[axis]) for axis in range(len(dims))]
    array = array.at[tuple(spot)].set(smallest)
    longest = dims.index(max(dims))
    spot[longest] = (spot[longest] + 1) % dims[longest]
    return array.at[tuple(spot)].set(high)


def level_of(rng, extent, pieces, smallest, largest):
    level, own = 1.0, jax.random.fold_in(rng, 6)
    for axis_at, shards_of in pieces:
        heights = jnp.exp(jax.random.uniform(jax.random.fold_in(own, axis_at), (shards_of,), jnp.float32, smallest / len(pieces), largest / len(pieces)))
        level = level * jnp.repeat(heights, extent[axis_at] // shards_of).reshape([-1 if axis == axis_at else 1 for axis in range(len(extent))])
    return level


def scatter_about(own_key, dims, width, most, shards=(), kind=jnp.bfloat16):
    drawn = width * jax.random.normal(own_key, dims, jnp.float32)
    if shards:
        drawn = drawn * level_of(own_key, dims, shards, -0.22, 0.18)
    return jnp.clip(drawn, -most, most).astype(kind)


def setup_inputs(seed: int = 0) -> dict:
    seeds = jax.random.split(jax.random.key(seed), 9)
    return {
        "window_rhs": scatter_about(seeds[0], (NRHS, WB * NB), 1.0, 6.0, ((1, 4),), jnp.float32),
        "past_solution": scatter_about(seeds[1], (NRHS, PAST * NB), 1.0, 6.0, ((1, 8),), jnp.float32),
        "past_panel": scatter_about(seeds[2], (WB * NB, PAST * NB), (PAST * NB) ** -0.5, 0.046875, ((0, 4), (1, 8)), jnp.float32),
        "window_panel": scatter_about(seeds[3], (WB, NB, COLS, NB), (4 * NB) ** -0.5, 0.09375, ((0, 4), (2, 8)), jnp.float32),
        "diag_inverse": draw_diag_inverse(jax.random.fold_in(seeds[8], 71), 0),
        "tile_list": touch_ends(jax.random.randint(seeds[5], (DEVICES, TPD), 0, TILES), jax.random.fold_in(seeds[5], 1), 0, TILES - 1).astype(jnp.int32),
        "neighbor_list": touch_ends(jax.random.randint(seeds[6], (DEVICES, TPD, NNB), 0, TILES), jax.random.fold_in(seeds[6], 1), 0, TILES - 1).astype(jnp.int32),
        "force_constants": scatter_about(seeds[7], (DEVICES, TPD, NNB, TILE, TILE), (NNB * TILE) ** -0.5, 0.1875, ((0, 32),), jnp.float32),
    }


def reference(window_rhs, past_solution, past_panel, window_panel, diag_inverse, tile_list, neighbor_list, force_constants):
    highest = lax.Precision.HIGHEST
    past_terms = jnp.dot(past_solution, past_panel.T, precision=highest, preferred_element_type=jnp.float32)
    solved = []
    for k in range(WB):
        total = past_terms[:, k * NB:(k + 1) * NB]
        for j in range(k):
            total = total + jnp.dot(solved[j], window_panel[k, :, j, :].T, precision=highest, preferred_element_type=jnp.float32)
        diff = window_rhs[:, k * NB:(k + 1) * NB] - total
        solved.append(jnp.dot(diff, diag_inverse[k].T, precision=highest, preferred_element_type=jnp.float32))
    solution = jnp.concatenate(solved, axis=1)
    tiles = solution.reshape(NRHS, TILES, TILE)
    rhs_tiles = window_rhs.reshape(NRHS, TILES, TILE)
    near = tiles[:, neighbor_list]
    term = jnp.einsum("rdtnb,dtnab->dtra", near, force_constants, precision=highest)
    own = jnp.transpose(rhs_tiles[:, tile_list], (1, 2, 0, 3))
    return solution, own - term
```

```python
import functools

import jax
import jax.numpy as jnp
from jax import lax
from jax.experimental import pallas as pl
from jax.experimental.pallas import tpu as pltpu
from jax.sharding import PartitionSpec as P

MESH = pl.DeviceIdType.MESH
BF16 = jnp.bfloat16
F32 = jnp.float32


def halves(value):
    high = value.astype(BF16)
    return high, (value - high.astype(F32)).astype(BF16)


def nt(left, right):
    return lax.dot_general(left, right, (((1,), (1,)), ((), ())), preferred_element_type=F32)


def nn(left, right):
    return lax.dot_general(left, right, (((1,), (0,)), ((), ())), preferred_element_type=F32)


def kernel(
    rows, cols, owners, tile, nrhs, tpd, nnb,
    rhs_hbm, psol_hbm, panel_hbm, win_hbm, dinv_hbm, tlist, nlist, force_hbm,
    sol_out, res_out,
    psol, panel, win, dinv, force, xpast, xx, whi, wlo, mhi, mlo, fhi, flo,
    part, rs_buf, diff, ubuf, vout, vbuf, y_all, rhs_all,
    load_sem, panel_sem, rhs_sem,
    rs_send, rs_recv, df_send, df_recv, sc_send, ln_send, ag_send, y_recv,
    rl_send, ra_send, r_recv, v_send, v_recv,
):
    p = lax.axis_index("prow")
    q = lax.axis_index("pcol")
    order = owners * tile
    owner = q < owners
    mine = lax.rem(q, owners)
    barrier = pltpu.get_barrier_semaphore()

    def at_plane(step):
        return lax.rem(q + 1 + step, cols)

    def at_line(step):
        return lax.rem(p + 1 + step, rows)

    def remote(src, dst, send, recv, row, col):
        return pltpu.make_async_remote_copy(
            src_ref=src, dst_ref=dst, send_sem=send, recv_sem=recv,
            device_id=(row, col), device_id_type=MESH,
        )

    def act(copy, go):
        if go:
            copy.start()
        else:
            copy.wait_send()

    first = pltpu.make_async_copy(psol_hbm, psol, load_sem.at[0])
    first.start()

    def panel_copy(c):
        at = pl.ds(pl.multiple_of(c * tile, tile), tile)
        return pltpu.make_async_copy(panel_hbm.at[at, :], panel.at[at, :], panel_sem.at[c])

    @pl.loop(0, owners)
    def _(i):
        panel_copy(lax.rem(q + 1 + i, owners)).start()

    def rhs_copy(c):
        return pltpu.make_async_copy(
            rhs_hbm.at[:, c * tile:(c + 1) * tile], rhs_all.at[p * owners + c], rhs_sem.at[c]
        )

    for c in range(owners):
        rhs_copy(c).start()
    load_dinv = pltpu.make_async_copy(dinv_hbm.at[0], dinv, load_sem.at[1])
    load_win = pltpu.make_async_copy(win_hbm.at[0, :, 0, :], win, load_sem.at[2])
    load_force = pltpu.make_async_copy(force_hbm.at[0], force, load_sem.at[3])
    load_dinv.start()
    load_win.start()
    load_force.start()

    @pl.loop(0, cols - 1)
    def _(i):
        pl.semaphore_signal(barrier, inc=1, device_id=(p, at_plane(i)), device_id_type=MESH)

    @pl.loop(0, rows - 1)
    def _(i):
        pl.semaphore_signal(barrier, inc=1, device_id=(at_line(i), q), device_id_type=MESH)

    first.wait()
    high, low = halves(psol[...])
    xpast[0:nrhs, :] = high
    xpast[nrhs:2 * nrhs, :] = low
    for c in range(owners):
        rhs_copy(c).wait()
    pl.semaphore_wait(barrier, cols - 1 + rows - 1)

    def rhs_line(go):
        t = p * owners + mine

        @pl.when(owner)
        def _():
            @pl.loop(0, rows - 1)
            def _(i):
                act(remote(rhs_all.at[t], rhs_all.at[t], rl_send.at[i], r_recv.at[t], at_line(i), q), go)

    rhs_line(True)

    def fold(value):
        turned = value.T
        return turned[:nrhs] + turned[nrhs:]

    def rs_copy(c):
        return remote(part.at[c], rs_buf.at[q], rs_send.at[c], rs_recv.at[q], p, c)

    @pl.loop(0, owners)
    def _(i):
        c = lax.rem(q + 1 + i, owners)
        panel_copy(c).wait()
        high, low = halves(panel[pl.ds(pl.multiple_of(c * tile, tile), tile), :])
        weights = xpast[...]
        part[c] = fold(nt(high, weights) + nt(low, weights))

        @pl.when(c != q)
        def _():
            rs_copy(c).start()

    load_dinv.wait()
    load_win.wait()

    @pl.when(q < p)
    def _():
        step = min(256, order)
        for at in range(0, order, step):
            high, low = halves(win[at:at + step, :])
            whi[at:at + step, :] = high
            wlo[at:at + step, :] = low
        for at in range(0, order, step):
            depth = at + step
            high, low = halves(dinv[at:at + step, :depth])
            value = nn(high, whi[:depth, :]) + nn(low, whi[:depth, :]) + nn(high, wlo[:depth, :])
            high, low = halves(value)
            mhi[at:at + step, :] = high
            mlo[at:at + step, :] = low

    def df_copy(i):
        return remote(diff.at[mine], diff.at[mine], df_send.at[i], df_recv.at[mine], p, at_plane(i))

    def df_all(go):
        @pl.when(owner)
        def _():
            @pl.loop(0, cols - 1)
            def _(i):
                d = at_plane(i)

                @pl.when(((p == 0) & (d < owners)) | (d == p - 1))
                def _():
                    act(df_copy(i), go)

    @pl.when(owner)
    def _():
        @pl.loop(0, cols - 1)
        def _(i):
            s = at_plane(i)
            remote(part.at[mine], rs_buf.at[s], rs_send.at[mine], rs_recv.at[s], p, s).wait_recv()

        total = part[mine]
        for i in range(cols - 1):
            total = total + rs_buf[at_plane(i)]
        diff[mine] = rhs_all[p * owners + mine] - total

    df_all(True)

    def pack(ref, base):
        for c in range(owners):
            high, low = halves(ref[base + c])
            xx[0:nrhs, c * tile:(c + 1) * tile] = high
            xx[nrhs:2 * nrhs, c * tile:(c + 1) * tile] = low

    def solve_tile(c):
        high, low = halves(dinv[pl.ds(pl.multiple_of(c * tile, tile), tile), :])
        weights = xx[...]
        return fold(nt(high, weights) + nt(low, weights))

    def df_wait():
        for c in range(owners):
            @pl.when(c != q)
            def _():
                remote(diff.at[c], diff.at[c], df_send.at[0], df_recv.at[c], p, at_plane(0)).wait_recv()

    def line_send(k, go):
        t = k * owners + mine

        @pl.when(owner)
        def _():
            @pl.loop(0, rows - 1)
            def _(i):
                act(remote(y_all.at[t], y_all.at[t], ln_send.at[i], y_recv.at[t], at_line(i), q), go)

    def plane_send(k, go):
        t = k * owners + mine

        @pl.when(owner)
        def _():
            @pl.loop(0, cols - 1)
            def _(i):
                d = at_plane(i)

                @pl.when((p != k) | (k == 0) | (d != k - 1))
                def _():
                    act(remote(y_all.at[t], y_all.at[t], ag_send.at[k, i], y_recv.at[t], p, d), go)

    def scatter(k, go):
        @pl.loop(0, owners)
        def _(i):
            c = lax.rem(q + 1 + i, owners)
            t = k * owners + c

            @pl.when(c != q)
            def _():
                act(remote(y_all.at[t], y_all.at[t], sc_send.at[c], y_recv.at[t], p, c), go)

    def y_wait(t):
        remote(y_all.at[t], y_all.at[t], ln_send.at[0], y_recv.at[t], p, at_plane(0)).wait_recv()

    def rhs_plane(go):
        @pl.when(owner)
        def _():
            @pl.loop(0, rows - 1)
            def _(j):
                t = at_line(j) * owners + mine
                if go:
                    remote(rhs_all.at[t], rhs_all.at[t], rl_send.at[0], r_recv.at[t], p, at_plane(0)).wait_recv()

                @pl.loop(0, cols - 1)
                def _(i):
                    act(remote(rhs_all.at[t], rhs_all.at[t], ra_send.at[j, i], r_recv.at[t], p, at_plane(i)), go)

    @pl.when(p == 0)
    def _():
        @pl.when(owner)
        def _():
            df_wait()
            pack(diff, 0)
            y_all[mine] = solve_tile(mine)

    @pl.when((p > 0) & (q == p - 1))
    def _():
        df_wait()
        pack(diff, 0)

        @pl.loop(0, owners)
        def _(c):
            ubuf[c] = solve_tile(c)

    def v_copy(j):
        return remote(vout, vbuf.at[j], v_send, v_recv.at[j], p, p - 1)

    load_force.wait()
    for t in range(tpd):
        for n in range(nnb):
            high, low = halves(force[t, n])
            fhi[t, :, n * tile:(n + 1) * tile] = high
            flo[t, :, n * tile:(n + 1) * tile] = low

    @pl.when(p >= 2)
    def _():
        rhs_plane(True)

    for k in range(rows):
        base = k * owners

        @pl.when(owner)
        def _():
            made = (p == k) if k == 0 else ((p == k) & (q == k - 1))

            @pl.when(jnp.logical_not(made))
            def _():
                y_wait(base + mine)

        @pl.when(p == k)
        def _():
            line_send(k, True)

        plane_send(k, True)

        @pl.when((p == k) & (p < 2))
        def _():
            rhs_plane(True)

        @pl.loop(0, cols - 1)
        def _(i):
            c = at_plane(i)

            @pl.when(c < owners)
            def _():
                if k == 0:
                    y_wait(base + c)
                else:
                    @pl.when((p != k) | (q != k - 1))
                    def _():
                        y_wait(base + c)

        if k < rows - 1:
            @pl.when((q == k) & (p > k))
            def _():
                pack(y_all, base)
                weights = xx[...]

                @pl.when(p == k + 1)
                def _():
                    for j in range(k):
                        remote(vout, vbuf.at[j], v_send, v_recv.at[j], p, at_plane(0)).wait_recv()

                    @pl.loop(0, owners)
                    def _(c):
                        at = pl.ds(pl.multiple_of(c * tile, tile), tile)
                        value = ubuf[c] - fold(nt(mhi[at, :], weights) + nt(mlo[at, :], weights))
                        for j in range(k):
                            value = value - vbuf[j, c]
                        y_all[(k + 1) * owners + c] = value

                        @pl.when(c != q)
                        def _():
                            t = (k + 1) * owners + c
                            remote(y_all.at[t], y_all.at[t], sc_send.at[c], y_recv.at[t], p, c).start()

                @pl.when(p > k + 1)
                def _():
                    @pl.loop(0, owners)
                    def _(c):
                        at = pl.ds(pl.multiple_of(c * tile, tile), tile)
                        vout[c] = fold(nt(mhi[at, :], weights) + nt(mlo[at, :], weights))

                    v_copy(k).start()

    for c in range(owners):
        sol_out[:, c * tile:(c + 1) * tile] = y_all[p * owners + c]

    @pl.loop(0, rows - 1)
    def _(j):
        @pl.loop(0, cols - 1)
        def _(i):
            c = at_plane(i)

            @pl.when(c < owners)
            def _():
                t = at_line(j) * owners + c
                remote(rhs_all.at[t], rhs_all.at[t], rl_send.at[0], r_recv.at[t], p, at_plane(0)).wait_recv()

    for t in range(tpd):
        for n in range(nnb):
            high, low = halves(y_all[nlist[0, t, n]])
            xx[0:nrhs, n * tile:(n + 1) * tile] = high
            xx[nrhs:2 * nrhs, n * tile:(n + 1) * tile] = low
        weights = xx[:, :nnb * tile]
        term = fold(nt(fhi[t], weights) + nt(flo[t], weights))
        res_out[0, t] = rhs_all[tlist[0, t]] - term

    rhs_line(False)

    @pl.loop(0, owners)
    def _(c):
        @pl.when(c != q)
        def _():
            rs_copy(c).wait_send()

    df_all(False)
    rhs_plane(False)
    for k in range(rows):
        @pl.when(p == k)
        def _():
            line_send(k, False)
            if k > 0:
                @pl.when(q == k - 1)
                def _():
                    scatter(k, False)

        plane_send(k, False)

    @pl.when(q < p - 1)
    def _():
        v_copy(q).wait_send()


def per_device(rows, cols, window_rhs, past_solution, past_panel, window_panel, diag_inverse, tile_list, neighbor_list, force_constants):
    nrhs, order = window_rhs.shape
    depth = past_solution.shape[1]
    tpd, nnb, tile = force_constants.shape[1:4]
    owners = order // tile
    tiles = rows * owners
    wide = max(order, nnb * tile)
    hbm = pl.BlockSpec(memory_space=pl.ANY)
    smem = pl.BlockSpec(memory_space=pltpu.SMEM)
    vmem = pl.BlockSpec(memory_space=pltpu.VMEM)
    dma = pltpu.SemaphoreType.DMA
    return pl.pallas_call(
        functools.partial(kernel, rows, cols, owners, tile, nrhs, tpd, nnb),
        out_shape=(
            jax.ShapeDtypeStruct((nrhs, order), F32),
            jax.ShapeDtypeStruct((1, tpd, nrhs, tile), F32),
        ),
        in_specs=[hbm, hbm, hbm, hbm, hbm, smem, smem, hbm],
        out_specs=(vmem, vmem),
        scratch_shapes=[
            pltpu.VMEM((nrhs, depth), F32),
            pltpu.VMEM((order, depth), F32),
            pltpu.VMEM((order, order), F32),
            pltpu.VMEM((order, order), F32),
            pltpu.VMEM((tpd, nnb, tile, tile), F32),
            pltpu.VMEM((2 * nrhs, depth), BF16),
            pltpu.VMEM((2 * nrhs, wide), BF16),
            pltpu.VMEM((order, order), BF16),
            pltpu.VMEM((order, order), BF16),
            pltpu.VMEM((order, order), BF16),
            pltpu.VMEM((order, order), BF16),
            pltpu.VMEM((tpd, tile, nnb * tile), BF16),
            pltpu.VMEM((tpd, tile, nnb * tile), BF16),
            pltpu.VMEM((owners, nrhs, tile), F32),
            pltpu.VMEM((cols, nrhs, tile), F32),
            pltpu.VMEM((owners, nrhs, tile), F32),
            pltpu.VMEM((owners, nrhs, tile), F32),
            pltpu.VMEM((owners, nrhs, tile), F32),
            pltpu.VMEM((max(rows - 2, 1), owners, nrhs, tile), F32),
            pltpu.VMEM((tiles, nrhs, tile), F32),
            pltpu.VMEM((tiles, nrhs, tile), F32),
            dma((4,)),
            dma((owners,)),
            dma((owners,)),
            dma((owners,)),
            dma((cols,)),
            dma((cols,)),
            dma((owners,)),
            dma((owners,)),
            dma((rows,)),
            dma((rows, cols)),
            dma((tiles,)),
            dma((rows,)),
            dma((rows, cols)),
            dma((tiles,)),
            dma,
            dma((rows,)),
        ],
        compiler_params=pltpu.CompilerParams(
            collective_id=0, has_side_effects=True, vmem_limit_bytes=52 * 2**20
        ),
    )(window_rhs, past_solution, past_panel, window_panel, diag_inverse, tile_list, neighbor_list, force_constants)


def solution(mesh):
    placed = (
        P(None, "prow"),
        P(None, "pcol"),
        P("prow", "pcol"),
        P("prow", None, "pcol", None),
        P("prow", None, None),
        P(("prow", "pcol"), None),
        P(("prow", "pcol"), None, None),
        P(("prow", "pcol"), None, None, None, None),
    )
    return jax.shard_map(
        functools.partial(per_device, mesh.shape["prow"], mesh.shape["pcol"]),
        mesh=mesh,
        in_specs=placed,
        out_specs=(P(None, "prow"), P(("prow", "pcol"), None, None, None)),
        check_vma=False,
    )
```

```python
import functools

import jax
import jax.numpy as jnp
from jax import lax
from jax.experimental import pallas as pl
from jax.experimental.pallas import tpu as pltpu
from jax.sharding import PartitionSpec as P

MESH = pl.DeviceIdType.MESH
BF16 = jnp.bfloat16
F32 = jnp.float32


def halves(value):
    high = value.astype(BF16)
    return high, (value - high.astype(F32)).astype(BF16)


def nt(left, right):
    return lax.dot_general(left, right, (((1,), (1,)), ((), ())), preferred_element_type=F32)


def nn(left, right):
    return lax.dot_general(left, right, (((1,), (0,)), ((), ())), preferred_element_type=F32)


def kernel(
    rows, cols, owners, tile, nrhs, tpd, nnb,
    rhs_hbm, psol_hbm, panel_hbm, win_hbm, dinv_hbm, tlist_hbm, nlist_hbm, force_hbm,
    sol_out, res_out,
    tlist, nlist, psol, panel, win, dinv, force, xpast, xx, whi, wlo, mhi, mlo, fhi, flo,
    part, rs_buf, outp, usend, ubuf, vout, vbuf, y_all, rhs_all,
    load_sem, panel_sem, rhs_sem,
    rs_send, rs_recv, df_send, df_recv, dx_send, ch_send, sc_send, ln_send, ag_send, y_recv,
    rl_send, ra_send, r_recv, v_send, v_recv,
):
    p = lax.axis_index("prow")
    q = lax.axis_index("pcol")
    order = owners * tile
    owner = q < owners
    mine = lax.rem(q, owners)
    barrier = pltpu.get_barrier_semaphore()

    def at_plane(step):
        return lax.rem(q + 1 + step, cols)

    def at_line(step):
        return lax.rem(p + 1 + step, rows)

    def remote(src, dst, send, recv, row, col):
        return pltpu.make_async_remote_copy(
            src_ref=src, dst_ref=dst, send_sem=send, recv_sem=recv,
            device_id=(row, col), device_id_type=MESH,
        )

    def act(copy, go):
        if go:
            copy.start()
        else:
            copy.wait_send()

    first = pltpu.make_async_copy(psol_hbm, psol, load_sem.at[0])
    first.start()

    def panel_copy(c):
        at = pl.ds(pl.multiple_of(c * tile, tile), tile)
        return pltpu.make_async_copy(panel_hbm.at[at, :], panel.at[at, :], panel_sem.at[c])

    @pl.loop(0, owners)
    def _(i):
        panel_copy(i).start()

    def rhs_copy(c):
        return pltpu.make_async_copy(
            rhs_hbm.at[:, c * tile:(c + 1) * tile], rhs_all.at[p * owners + c], rhs_sem.at[c]
        )

    for c in range(owners):
        rhs_copy(c).start()
    load_dinv = pltpu.make_async_copy(dinv_hbm.at[0], dinv, load_sem.at[1])
    load_win = pltpu.make_async_copy(win_hbm.at[0, :, 0, :], win, load_sem.at[2])
    load_force = pltpu.make_async_copy(force_hbm.at[0], force, load_sem.at[3])
    load_tlist = pltpu.make_async_copy(tlist_hbm, tlist, load_sem.at[4])
    load_nlist = pltpu.make_async_copy(nlist_hbm, nlist, load_sem.at[5])
    load_dinv.start()
    load_tlist.start()
    load_nlist.start()

    @pl.loop(0, cols - 1)
    def _(i):
        pl.semaphore_signal(barrier, inc=1, device_id=(p, at_plane(i)), device_id_type=MESH)

    @pl.loop(0, rows - 1)
    def _(i):
        pl.semaphore_signal(barrier, inc=1, device_id=(at_line(i), q), device_id_type=MESH)

    @pl.when((p >= 2) & (q == p - 1))
    def _():
        pl.semaphore_signal(barrier, inc=1, device_id=(p - 1, q - 1), device_id_type=MESH)

    @pl.when((p == 1) & (q == 0))
    def _():
        @pl.loop(1, owners)
        def _(c):
            pl.semaphore_signal(barrier, inc=1, device_id=(0, c), device_id_type=MESH)

    first.wait()
    high, low = halves(psol[...])
    xpast[0:nrhs, :] = high
    xpast[nrhs:2 * nrhs, :] = low
    for c in range(owners):
        rhs_copy(c).wait()
    passes_on = ((p == 0) & owner & (q > 0)) | ((p > 0) & (p < rows - 1) & (q == p - 1))
    pl.semaphore_wait(barrier, cols - 1 + rows - 1 + jnp.where(passes_on, 1, 0))

    def rhs_line(go):
        t = p * owners + mine

        @pl.when(owner)
        def _():
            @pl.loop(0, rows - 1)
            def _(i):
                act(remote(rhs_all.at[t], rhs_all.at[t], rl_send.at[i], r_recv.at[t], at_line(i), q), go)

    rhs_line(True)

    def fold(value):
        turned = value.T
        return turned[:nrhs] + turned[nrhs:]

    def pack(ref, base):
        for c in range(owners):
            high, low = halves(ref[base + c])
            xx[0:nrhs, c * tile:(c + 1) * tile] = high
            xx[nrhs:2 * nrhs, c * tile:(c + 1) * tile] = low

    def rs_copy(c):
        return remote(outp.at[c], rs_buf.at[q], rs_send.at[c], rs_recv.at[q], p, c)

    step = min(256, order)
    pair = step // tile

    @pl.loop(0, order // step)
    def _(i):
        for n in range(pair):
            panel_copy(i * pair + n).wait()
        high, low = halves(panel[pl.ds(pl.multiple_of(i * step, step), step), :])
        weights = xpast[...]
        value = nt(high, weights) + nt(low, weights)
        for n in range(pair):
            part[i * pair + n] = fold(value[n * tile:(n + 1) * tile])

    load_win.start()
    load_force.start()

    @pl.when(q == 0)
    def _():
        for c in range(owners):
            part[c] = part[c] - rhs_all[p * owners + c]

    load_dinv.wait()
    pack(part, 0)
    for at in range(0, order, step):
        depth = at + step
        high, low = halves(dinv[at:depth, :depth])
        weights = xx[:, :depth]
        value = nt(high, weights) + nt(low, weights)
        for n in range(pair):
            c = at // tile + n
            outp[c] = fold(value[n * tile:(n + 1) * tile])

            @pl.when(c != q)
            def _():
                rs_copy(c).start()

    load_win.wait()

    @pl.when(q < p)
    def _():
        for at in range(0, order, step):
            high, low = halves(win[at:at + step, :])
            whi[at:at + step, :] = high
            wlo[at:at + step, :] = low
        for at in range(0, order, step):
            depth = at + step
            high, low = halves(dinv[at:at + step, :depth])
            value = nn(high, whi[:depth, :]) + nn(low, whi[:depth, :]) + nn(high, wlo[:depth, :])
            high, low = halves(value)
            mhi[at:at + step, :] = high
            mlo[at:at + step, :] = low

    solver = (p > 0) & (q == p - 1)

    def df_send_one(go):
        @pl.when(owner & (p > 0) & jnp.logical_not(solver))
        def _():
            act(remote(usend, ubuf.at[mine], df_send, df_recv.at[mine], p, p - 1), go)

    def first_send(go):
        @pl.when(owner & (p == 0))
        def _():
            act(remote(y_all.at[mine], y_all.at[mine], dx_send.at[mine], y_recv.at[mine], 1, 0), go)

    def line_send(k, go):
        t = k * owners + mine

        @pl.when(owner)
        def _():
            @pl.loop(0, rows - 1)
            def _(i):
                @pl.when((q != k) | (at_line(i) < k))
                def _():
                    act(remote(y_all.at[t], y_all.at[t], ln_send.at[i], y_recv.at[t], at_line(i), q), go)

    def has_whole(k, row, col):
        handed = (row > k) & (col == k)
        return handed if k == 0 else handed | ((row == k) & (col == k - 1))

    def plane_send(k, go):
        t = k * owners + mine

        @pl.when(owner)
        def _():
            @pl.loop(0, cols - 1)
            def _(i):
                d = at_plane(i)

                @pl.when(jnp.logical_not(has_whole(k, p, d)))
                def _():
                    act(remote(y_all.at[t], y_all.at[t], ag_send.at[k, i], y_recv.at[t], p, d), go)

    def solved_send(k, c, go):
        t = k * owners + c
        if k < rows - 1:
            act(remote(y_all.at[t], y_all.at[t], dx_send.at[c], y_recv.at[t], p + 1, k), go)

        @pl.when(c != q)
        def _():
            act(remote(y_all.at[t], y_all.at[t], sc_send.at[c], y_recv.at[t], p, c), go)

    def chain_send(k, c, go):
        t = k * owners + c

        @pl.when(p < rows - 1)
        def _():
            act(remote(y_all.at[t], y_all.at[t], ch_send.at[c], y_recv.at[t], p + 1, q), go)

    def v_send_one(j, c, go):
        act(remote(vout.at[c], vbuf.at[j, c], v_send.at[c], v_recv.at[j, c], p, p - 1), go)

    def y_wait(t):
        remote(y_all.at[t], y_all.at[t], ln_send.at[0], y_recv.at[t], p, at_plane(0)).wait_recv()

    def rhs_plane(go):
        @pl.when(owner)
        def _():
            @pl.loop(0, rows - 1)
            def _(j):
                t = at_line(j) * owners + mine
                if go:
                    remote(rhs_all.at[t], rhs_all.at[t], rl_send.at[0], r_recv.at[t], p, at_plane(0)).wait_recv()

                @pl.loop(0, cols - 1)
                def _(i):
                    act(remote(rhs_all.at[t], rhs_all.at[t], ra_send.at[j, i], r_recv.at[t], p, at_plane(i)), go)

    @pl.when(owner)
    def _():
        @pl.loop(0, cols - 1)
        def _(i):
            s = at_plane(i)
            remote(outp.at[mine], rs_buf.at[s], rs_send.at[mine], rs_recv.at[s], p, s).wait_recv()

        total = outp[mine]
        for i in range(cols - 1):
            total = total + rs_buf[at_plane(i)]

        @pl.when(p == 0)
        def _():
            y_all[mine] = -total

        @pl.when(solver)
        def _():
            ubuf[mine] = -total

        @pl.when((p > 0) & jnp.logical_not(solver))
        def _():
            usend[...] = -total

    first_send(True)
    df_send_one(True)

    @pl.when(p >= 2)
    def _():
        rhs_plane(True)

    @pl.when(solver)
    def _():
        for c in range(owners):
            @pl.when(c != q)
            def _():
                remote(usend, ubuf.at[c], df_send, df_recv.at[c], p, at_plane(0)).wait_recv()

    for k in range(rows):
        base = k * owners
        handed = (p > k) & (q == k)
        made = p == k if k == 0 else (p == k) & (q == k - 1)

        @pl.when(handed)
        def _():
            @pl.loop(0, owners)
            def _(c):
                y_wait(base + c)
                chain_send(k, c, True)

            pack(y_all, base)
            weights = xx[...]

            def product(c):
                at = pl.ds(pl.multiple_of(c * tile, tile), tile)
                return fold(nt(mhi[at, :], weights) + nt(mlo[at, :], weights))

            @pl.when(p == k + 1)
            def _():
                for j in range(k):
                    @pl.loop(0, owners)
                    def _(c):
                        remote(vout.at[c], vbuf.at[j, c], v_send.at[c], v_recv.at[j, c], p, at_plane(0)).wait_recv()

                @pl.loop(0, owners)
                def _(c):
                    value = ubuf[c] - product(c)
                    for j in range(k):
                        value = value - vbuf[j, c]
                    y_all[base + owners + c] = value
                    if k < rows - 1:
                        solved_send(k + 1, c, True)

            @pl.when(p > k + 1)
            def _():
                @pl.loop(0, owners)
                def _(c):
                    vout[c] = product(c)
                    v_send_one(k, c, True)

        @pl.when(owner & jnp.logical_not(made | handed))
        def _():
            y_wait(base + mine)

        @pl.when(p == k)
        def _():
            line_send(k, True)

        plane_send(k, True)

        @pl.when((p == k) & (p < 2))
        def _():
            rhs_plane(True)

    load_force.wait()
    for t in range(tpd):
        for n in range(nnb):
            high, low = halves(force[t, n])
            fhi[t, :, n * tile:(n + 1) * tile] = high
            flo[t, :, n * tile:(n + 1) * tile] = low

    for k in range(rows):
        @pl.when(jnp.logical_not(has_whole(k, p, q)))
        def _():
            @pl.loop(0, cols - 1)
            def _(i):
                c = at_plane(i)

                @pl.when(c < owners)
                def _():
                    y_wait(k * owners + c)

    for c in range(owners):
        sol_out[:, c * tile:(c + 1) * tile] = y_all[p * owners + c]

    load_tlist.wait()
    load_nlist.wait()

    @pl.loop(0, rows - 1)
    def _(j):
        @pl.loop(0, cols - 1)
        def _(i):
            c = at_plane(i)

            @pl.when(c < owners)
            def _():
                t = at_line(j) * owners + c
                remote(rhs_all.at[t], rhs_all.at[t], rl_send.at[0], r_recv.at[t], p, at_plane(0)).wait_recv()

    for t in range(tpd):
        for n in range(nnb):
            high, low = halves(y_all[nlist[0, t, n]])
            xx[0:nrhs, n * tile:(n + 1) * tile] = high
            xx[nrhs:2 * nrhs, n * tile:(n + 1) * tile] = low
        weights = xx[:, :nnb * tile]
        term = fold(nt(fhi[t], weights) + nt(flo[t], weights))
        res_out[0, t] = rhs_all[tlist[0, t]] - term

    rhs_line(False)

    @pl.loop(0, owners)
    def _(c):
        @pl.when(c != q)
        def _():
            rs_copy(c).wait_send()

    first_send(False)
    df_send_one(False)
    rhs_plane(False)
    for k in range(rows):
        @pl.when(p == k)
        def _():
            line_send(k, False)

        if k > 0:
            @pl.when((p == k) & (q == k - 1))
            def _():
                @pl.loop(0, owners)
                def _(c):
                    solved_send(k, c, False)

        @pl.when((p > k) & (q == k))
        def _():
            @pl.loop(0, owners)
            def _(c):
                chain_send(k, c, False)

                @pl.when(p > k + 1)
                def _():
                    v_send_one(k, c, False)

        plane_send(k, False)


def per_device(rows, cols, window_rhs, past_solution, past_panel, window_panel, diag_inverse, tile_list, neighbor_list, force_constants):
    nrhs, order = window_rhs.shape
    depth = past_solution.shape[1]
    tpd, nnb, tile = force_constants.shape[1:4]
    owners = order // tile
    tiles = rows * owners
    wide = max(order, nnb * tile)
    hbm = pl.BlockSpec(memory_space=pltpu.HBM)
    vmem = pl.BlockSpec(memory_space=pltpu.VMEM)
    dma = pltpu.SemaphoreType.DMA
    return pl.pallas_call(
        functools.partial(kernel, rows, cols, owners, tile, nrhs, tpd, nnb),
        out_shape=(
            jax.ShapeDtypeStruct((nrhs, order), F32),
            jax.ShapeDtypeStruct((1, tpd, nrhs, tile), F32),
        ),
        in_specs=[hbm] * 8,
        out_specs=(vmem, vmem),
        scratch_shapes=[
            pltpu.SMEM((1, tpd), jnp.int32),
            pltpu.SMEM((1, tpd, nnb), jnp.int32),
            pltpu.VMEM((nrhs, depth), F32),
            pltpu.VMEM((order, depth), F32),
            pltpu.VMEM((order, order), F32),
            pltpu.VMEM((order, order), F32),
            pltpu.VMEM((tpd, nnb, tile, tile), F32),
            pltpu.VMEM((2 * nrhs, depth), BF16),
            pltpu.VMEM((2 * nrhs, wide), BF16),
            pltpu.VMEM((order, order), BF16),
            pltpu.VMEM((order, order), BF16),
            pltpu.VMEM((order, order), BF16),
            pltpu.VMEM((order, order), BF16),
            pltpu.VMEM((tpd, tile, nnb * tile), BF16),
            pltpu.VMEM((tpd, tile, nnb * tile), BF16),
            pltpu.VMEM((owners, nrhs, tile), F32),
            pltpu.VMEM((cols, nrhs, tile), F32),
            pltpu.VMEM((owners, nrhs, tile), F32),
            pltpu.VMEM((nrhs, tile), F32),
            pltpu.VMEM((owners, nrhs, tile), F32),
            pltpu.VMEM((owners, nrhs, tile), F32),
            pltpu.VMEM((max(rows - 2, 1), owners, nrhs, tile), F32),
            pltpu.VMEM((tiles, nrhs, tile), F32),
            pltpu.VMEM((tiles, nrhs, tile), F32),
            dma((6,)),
            dma((owners,)),
            dma((owners,)),
            dma((owners,)),
            dma((cols,)),
            dma,
            dma((owners,)),
            dma((owners,)),
            dma((owners,)),
            dma((owners,)),
            dma((rows,)),
            dma((rows, cols)),
            dma((tiles,)),
            dma((rows,)),
            dma((rows, cols)),
            dma((tiles,)),
            dma((owners,)),
            dma((rows, owners)),
        ],
        compiler_params=pltpu.CompilerParams(
            collective_id=0, has_side_effects=True, vmem_limit_bytes=63 * 2**20
        ),
    )(window_rhs, past_solution, past_panel, window_panel, diag_inverse, tile_list, neighbor_list, force_constants)


def solution(mesh):
    placed = (
        P(None, "prow"),
        P(None, "pcol"),
        P("prow", "pcol"),
        P("prow", None, "pcol", None),
        P("prow", None, None),
        P(("prow", "pcol"), None),
        P(("prow", "pcol"), None, None),
        P(("prow", "pcol"), None, None, None, None),
    )
    return jax.shard_map(
        functools.partial(per_device, mesh.shape["prow"], mesh.shape["pcol"]),
        mesh=mesh,
        in_specs=placed,
        out_specs=(P(None, "prow"), P(("prow", "pcol"), None, None, None)),
        check_vma=False,
    )
```

```python
import functools

import jax
import jax.numpy as jnp
from jax import lax
from jax.experimental import pallas as pl
from jax.experimental.pallas import tpu as pltpu
from jax.sharding import PartitionSpec as P

MESH = pl.DeviceIdType.MESH
BF16 = jnp.bfloat16
F32 = jnp.float32


def halves(value):
    high = value.astype(BF16)
    return high, (value - high.astype(F32)).astype(BF16)


def nn(left, right):
    return lax.dot_general(left, right, (((1,), (0,)), ((), ())), preferred_element_type=F32)


def turned(block):
    high = block.astype(BF16).astype(F32)
    return jnp.concatenate([high, block - high], axis=0).T.astype(BF16)


def kernel(
    rows, cols, owners, tile, nrhs, tpd, nnb,
    rhs_hbm, psol_hbm, panel_hbm, win_hbm, dinv_hbm, tlist_hbm, nlist_hbm, force_hbm,
    sol_out, res_out,
    tlist, nlist, psol, panel, win, dinv, force, xpast, xx, whi, wlo, mhi, mlo, fhi, flo,
    part, rs_buf, outp, usend, ubuf, vout, vbuf, y_all, rhs_all,
    load_sem, panel_sem, rhs_sem,
    rs_send, rs_recv, df_send, df_recv, dx_send, ch_send, sc_send, ln_send, ag_send, y_recv,
    rl_send, ra_send, r_recv, v_send, v_recv,
):
    p = lax.axis_index("prow")
    q = lax.axis_index("pcol")
    order = owners * tile
    owner = q < owners
    mine = lax.rem(q, owners)
    barrier = pltpu.get_barrier_semaphore()

    def at_plane(step):
        return lax.rem(q + 1 + step, cols)

    def at_line(step):
        return lax.rem(p + 1 + step, rows)

    def remote(src, dst, send, recv, row, col):
        return pltpu.make_async_remote_copy(
            src_ref=src, dst_ref=dst, send_sem=send, recv_sem=recv,
            device_id=(row, col), device_id_type=MESH,
        )

    def act(copy, go):
        if go:
            copy.start()
        else:
            copy.wait_send()

    first = pltpu.make_async_copy(psol_hbm, psol, load_sem.at[0])
    first.start()

    def panel_copy(c):
        at = pl.ds(pl.multiple_of(c * tile, tile), tile)
        return pltpu.make_async_copy(panel_hbm.at[at, :], panel.at[at, :], panel_sem.at[c])

    @pl.loop(0, owners)
    def _(i):
        panel_copy(i).start()

    def rhs_copy(c):
        return pltpu.make_async_copy(
            rhs_hbm.at[:, c * tile:(c + 1) * tile], rhs_all.at[p * owners + c], rhs_sem.at[c]
        )

    for c in range(owners):
        rhs_copy(c).start()
    load_dinv = pltpu.make_async_copy(dinv_hbm.at[0], dinv, load_sem.at[1])
    load_win = pltpu.make_async_copy(win_hbm.at[0, :, 0, :], win, load_sem.at[2])
    load_force = pltpu.make_async_copy(force_hbm.at[0], force, load_sem.at[3])
    load_tlist = pltpu.make_async_copy(tlist_hbm, tlist, load_sem.at[4])
    load_nlist = pltpu.make_async_copy(nlist_hbm, nlist, load_sem.at[5])
    @pl.when(q < p)
    def _():
        load_win.start()

    load_dinv.start()
    load_tlist.start()
    load_nlist.start()

    @pl.loop(0, cols - 1)
    def _(i):
        pl.semaphore_signal(barrier, inc=1, device_id=(p, at_plane(i)), device_id_type=MESH)

    @pl.loop(0, rows - 1)
    def _(i):
        pl.semaphore_signal(barrier, inc=1, device_id=(at_line(i), q), device_id_type=MESH)

    @pl.when((p >= 2) & (q == p - 1))
    def _():
        pl.semaphore_signal(barrier, inc=1, device_id=(p - 1, q - 1), device_id_type=MESH)

    @pl.when((p == 1) & (q == 0))
    def _():
        @pl.loop(1, owners)
        def _(c):
            pl.semaphore_signal(barrier, inc=1, device_id=(0, c), device_id_type=MESH)

    first.wait()
    for at in range(0, psol.shape[1], tile):
        xpast[at:at + tile, :] = turned(psol[:, at:at + tile])
    for c in range(owners):
        rhs_copy(c).wait()
    passes_on = ((p == 0) & owner & (q > 0)) | ((p > 0) & (p < rows - 1) & (q == p - 1))
    pl.semaphore_wait(barrier, cols - 1 + rows - 1 + jnp.where(passes_on, 1, 0))

    def rhs_line(go):
        t = p * owners + mine

        @pl.when(owner)
        def _():
            @pl.loop(0, rows - 1)
            def _(i):
                act(remote(rhs_all.at[t], rhs_all.at[t], rl_send.at[i], r_recv.at[t], at_line(i), q), go)

    rhs_line(True)

    def fold(value):
        turned = value.T
        return turned[:nrhs] + turned[nrhs:]

    def pack(ref, base):
        for c in range(owners):
            xx[c * tile:(c + 1) * tile, :] = turned(ref[base + c])

    def rs_copy(c):
        return remote(outp.at[c], rs_buf.at[q], rs_send.at[c], rs_recv.at[q], p, c)

    step = min(256, order)
    pair = step // tile

    @pl.loop(0, order // step)
    def _(i):
        for n in range(pair):
            panel_copy(i * pair + n).wait()
        high, low = halves(panel[pl.ds(pl.multiple_of(i * step, step), step), :])
        weights = xpast[...]
        value = nn(high, weights) + nn(low, weights)
        for n in range(pair):
            part[i * pair + n] = fold(value[n * tile:(n + 1) * tile])

    load_force.start()

    @pl.when(q == 0)
    def _():
        for c in range(owners):
            part[c] = part[c] - rhs_all[p * owners + c]

    load_dinv.wait()
    pack(part, 0)
    for at in range(0, order, step):
        depth = at + step
        high, low = halves(dinv[at:depth, :depth])
        weights = xx[:depth, :]
        value = nn(high, weights) + nn(low, weights)
        for n in range(pair):
            c = at // tile + n
            outp[c] = fold(value[n * tile:(n + 1) * tile])

            @pl.when(c != q)
            def _():
                rs_copy(c).start()

    @pl.when(q < p)
    def _():
        load_win.wait()
        for at in range(0, order, step):
            high, low = halves(win[at:at + step, :])
            whi[at:at + step, :] = high
            wlo[at:at + step, :] = low
        for at in range(0, order, step):
            depth = at + step
            high, low = halves(dinv[at:at + step, :depth])
            value = nn(high, whi[:depth, :]) + nn(low, whi[:depth, :]) + nn(high, wlo[:depth, :])
            high, low = halves(value)
            mhi[at:at + step, :] = high
            mlo[at:at + step, :] = low

    solver = (p > 0) & (q == p - 1)

    def df_send_one(go):
        @pl.when(owner & (p > 0) & jnp.logical_not(solver))
        def _():
            act(remote(usend, ubuf.at[mine], df_send, df_recv.at[mine], p, p - 1), go)

    def first_send(go):
        @pl.when(owner & (p == 0))
        def _():
            act(remote(y_all.at[mine], y_all.at[mine], dx_send.at[mine], y_recv.at[mine], 1, 0), go)

    def line_send(k, go):
        t = k * owners + mine

        @pl.when(owner)
        def _():
            @pl.loop(0, rows - 1)
            def _(i):
                @pl.when((q != k) | (at_line(i) < k))
                def _():
                    act(remote(y_all.at[t], y_all.at[t], ln_send.at[i], y_recv.at[t], at_line(i), q), go)

    def has_whole(k, row, col):
        handed = (row > k) & (col == k)
        return handed if k == 0 else handed | ((row == k) & (col == k - 1))

    def plane_send(k, go):
        t = k * owners + mine

        @pl.when(owner)
        def _():
            @pl.loop(0, cols - 1)
            def _(i):
                d = at_plane(i)

                @pl.when(jnp.logical_not(has_whole(k, p, d)))
                def _():
                    act(remote(y_all.at[t], y_all.at[t], ag_send.at[k, i], y_recv.at[t], p, d), go)

    def solved_send(k, c, go):
        t = k * owners + c
        if k < rows - 1:
            act(remote(y_all.at[t], y_all.at[t], dx_send.at[c], y_recv.at[t], p + 1, k), go)

        @pl.when(c != q)
        def _():
            act(remote(y_all.at[t], y_all.at[t], sc_send.at[c], y_recv.at[t], p, c), go)

    def chain_send(k, c, go):
        t = k * owners + c

        @pl.when(p < rows - 1)
        def _():
            act(remote(y_all.at[t], y_all.at[t], ch_send.at[c], y_recv.at[t], p + 1, q), go)

    def v_send_one(j, c, go):
        act(remote(vout.at[c], vbuf.at[j, c], v_send.at[c], v_recv.at[j, c], p, p - 1), go)

    def y_wait(t):
        remote(y_all.at[t], y_all.at[t], ln_send.at[0], y_recv.at[t], p, at_plane(0)).wait_recv()

    def rhs_plane(go):
        @pl.when(owner)
        def _():
            @pl.loop(0, rows - 1)
            def _(j):
                t = at_line(j) * owners + mine
                if go:
                    remote(rhs_all.at[t], rhs_all.at[t], rl_send.at[0], r_recv.at[t], p, at_plane(0)).wait_recv()

                @pl.loop(0, cols - 1)
                def _(i):
                    act(remote(rhs_all.at[t], rhs_all.at[t], ra_send.at[j, i], r_recv.at[t], p, at_plane(i)), go)

    @pl.when(owner)
    def _():
        @pl.loop(0, cols - 1)
        def _(i):
            s = at_plane(i)
            remote(outp.at[mine], rs_buf.at[s], rs_send.at[mine], rs_recv.at[s], p, s).wait_recv()

        total = outp[mine]
        for i in range(cols - 1):
            total = total + rs_buf[at_plane(i)]

        @pl.when(p == 0)
        def _():
            y_all[mine] = -total

        @pl.when(solver)
        def _():
            ubuf[mine] = -total

        @pl.when((p > 0) & jnp.logical_not(solver))
        def _():
            usend[...] = -total

    first_send(True)
    df_send_one(True)

    @pl.when(p >= 2)
    def _():
        rhs_plane(True)

    @pl.when(solver)
    def _():
        for c in range(owners):
            @pl.when(c != q)
            def _():
                remote(usend, ubuf.at[c], df_send, df_recv.at[c], p, at_plane(0)).wait_recv()

    for k in range(rows):
        base = k * owners
        handed = (p > k) & (q == k)
        made = p == k if k == 0 else (p == k) & (q == k - 1)

        @pl.when(handed)
        def _():
            for c in range(owners):
                y_wait(base + c)
                chain_send(k, c, True)
                xx[c * tile:(c + 1) * tile, :] = turned(y_all[base + c])

            def product(at):
                weights = xx[:order, :]
                return nn(mhi[at:at + step, :], weights) + nn(mlo[at:at + step, :], weights)

            @pl.when(p == k + 1)
            def _():
                for j in range(k):
                    @pl.loop(0, owners)
                    def _(c):
                        remote(vout.at[c], vbuf.at[j, c], v_send.at[c], v_recv.at[j, c], p, at_plane(0)).wait_recv()

                for at in range(0, order, step):
                    whole = product(at)
                    for n in range(pair):
                        c = at // tile + n
                        value = ubuf[c] - fold(whole[n * tile:(n + 1) * tile])
                        for j in range(k):
                            value = value - vbuf[j, c]
                        y_all[base + owners + c] = value
                        if k < rows - 1:
                            solved_send(k + 1, c, True)

            @pl.when(p > k + 1)
            def _():
                for at in range(0, order, step):
                    whole = product(at)
                    for n in range(pair):
                        c = at // tile + n
                        vout[c] = fold(whole[n * tile:(n + 1) * tile])
                        v_send_one(k, c, True)

        @pl.when(owner & jnp.logical_not(made | handed))
        def _():
            y_wait(base + mine)

        @pl.when(p == k)
        def _():
            line_send(k, True)

        plane_send(k, True)

        @pl.when((p == k) & (p < 2))
        def _():
            rhs_plane(True)

    load_force.wait()
    for t in range(tpd):
        for n in range(nnb):
            high, low = halves(force[t, n])
            fhi[t, :, n * tile:(n + 1) * tile] = high
            flo[t, :, n * tile:(n + 1) * tile] = low

    for k in range(rows):
        @pl.when(jnp.logical_not(has_whole(k, p, q)))
        def _():
            @pl.loop(0, cols - 1)
            def _(i):
                c = at_plane(i)

                @pl.when(c < owners)
                def _():
                    y_wait(k * owners + c)

    for c in range(owners):
        sol_out[:, c * tile:(c + 1) * tile] = y_all[p * owners + c]

    load_tlist.wait()
    load_nlist.wait()

    @pl.loop(0, rows - 1)
    def _(j):
        @pl.loop(0, cols - 1)
        def _(i):
            c = at_plane(i)

            @pl.when(c < owners)
            def _():
                t = at_line(j) * owners + c
                remote(rhs_all.at[t], rhs_all.at[t], rl_send.at[0], r_recv.at[t], p, at_plane(0)).wait_recv()

    for t in range(tpd):
        weights = jnp.concatenate([turned(y_all[nlist[0, t, n]]) for n in range(nnb)], axis=0)
        term = fold(nn(fhi[t], weights) + nn(flo[t], weights))
        res_out[0, t] = rhs_all[tlist[0, t]] - term

    rhs_line(False)

    @pl.loop(0, owners)
    def _(c):
        @pl.when(c != q)
        def _():
            rs_copy(c).wait_send()

    first_send(False)
    df_send_one(False)
    rhs_plane(False)
    for k in range(rows):
        @pl.when(p == k)
        def _():
            line_send(k, False)

        if k > 0:
            @pl.when((p == k) & (q == k - 1))
            def _():
                @pl.loop(0, owners)
                def _(c):
                    solved_send(k, c, False)

        @pl.when((p > k) & (q == k))
        def _():
            @pl.loop(0, owners)
            def _(c):
                chain_send(k, c, False)

                @pl.when(p > k + 1)
                def _():
                    v_send_one(k, c, False)

        plane_send(k, False)


def per_device(rows, cols, window_rhs, past_solution, past_panel, window_panel, diag_inverse, tile_list, neighbor_list, force_constants):
    nrhs, order = window_rhs.shape
    depth = past_solution.shape[1]
    tpd, nnb, tile = force_constants.shape[1:4]
    owners = order // tile
    tiles = rows * owners
    hbm = pl.BlockSpec(memory_space=pltpu.HBM)
    vmem = pl.BlockSpec(memory_space=pltpu.VMEM)
    dma = pltpu.SemaphoreType.DMA
    return pl.pallas_call(
        functools.partial(kernel, rows, cols, owners, tile, nrhs, tpd, nnb),
        out_shape=(
            jax.ShapeDtypeStruct((nrhs, order), F32),
            jax.ShapeDtypeStruct((1, tpd, nrhs, tile), F32),
        ),
        in_specs=[hbm] * 8,
        out_specs=(vmem, vmem),
        scratch_shapes=[
            pltpu.SMEM((1, tpd), jnp.int32),
            pltpu.SMEM((1, tpd, nnb), jnp.int32),
            pltpu.VMEM((nrhs, depth), F32),
            pltpu.VMEM((order, depth), F32),
            pltpu.VMEM((order, order), F32),
            pltpu.VMEM((order, order), F32),
            pltpu.VMEM((tpd, nnb, tile, tile), F32),
            pltpu.VMEM((depth, 2 * nrhs), BF16),
            pltpu.VMEM((order, 2 * nrhs), BF16),
            pltpu.VMEM((order, order), BF16),
            pltpu.VMEM((order, order), BF16),
            pltpu.VMEM((order, order), BF16),
            pltpu.VMEM((order, order), BF16),
            pltpu.VMEM((tpd, tile, nnb * tile), BF16),
            pltpu.VMEM((tpd, tile, nnb * tile), BF16),
            pltpu.VMEM((owners, nrhs, tile), F32),
            pltpu.VMEM((cols, nrhs, tile), F32),
            pltpu.VMEM((owners, nrhs, tile), F32),
            pltpu.VMEM((nrhs, tile), F32),
            pltpu.VMEM((owners, nrhs, tile), F32),
            pltpu.VMEM((owners, nrhs, tile), F32),
            pltpu.VMEM((max(rows - 2, 1), owners, nrhs, tile), F32),
            pltpu.VMEM((tiles, nrhs, tile), F32),
            pltpu.VMEM((tiles, nrhs, tile), F32),
            dma((6,)),
            dma((owners,)),
            dma((owners,)),
            dma((owners,)),
            dma((cols,)),
            dma,
            dma((owners,)),
            dma((owners,)),
            dma((owners,)),
            dma((owners,)),
            dma((rows,)),
            dma((rows, cols)),
            dma((tiles,)),
            dma((rows,)),
            dma((rows, cols)),
            dma((tiles,)),
            dma((owners,)),
            dma((rows, owners)),
        ],
        compiler_params=pltpu.CompilerParams(
            collective_id=0, has_side_effects=True, vmem_limit_bytes=63 * 2**20
        ),
    )(window_rhs, past_solution, past_panel, window_panel, diag_inverse, tile_list, neighbor_list, force_constants)


def solution(mesh):
    placed = (
        P(None, "prow"),
        P(None, "pcol"),
        P("prow", "pcol"),
        P("prow", None, "pcol", None),
        P("prow", None, None),
        P(("prow", "pcol"), None),
        P(("prow", "pcol"), None, None),
        P(("prow", "pcol"), None, None, None, None),
    )
    return jax.shard_map(
        functools.partial(per_device, mesh.shape["prow"], mesh.shape["pcol"]),
        mesh=mesh,
        in_specs=placed,
        out_specs=(P(None, "prow"), P(("prow", "pcol"), None, None, None)),
        check_vma=False,
    )
```

```python
import functools

import jax
import jax.numpy as jnp
from jax import lax
from jax.experimental import pallas as pl
from jax.experimental.pallas import tpu as pltpu
from jax.sharding import PartitionSpec as P

MESH = pl.DeviceIdType.MESH
BF16 = jnp.bfloat16
F32 = jnp.float32


def halves(value):
    high = value.astype(BF16)
    return high, (value - high.astype(F32)).astype(BF16)


def nn(left, right):
    return lax.dot_general(left, right, (((1,), (0,)), ((), ())), preferred_element_type=F32)


def turned(block):
    high = block.astype(BF16).astype(F32)
    return jnp.concatenate([high, block - high], axis=0).T.astype(BF16)


def kernel(
    rows, cols, owners, tile, nrhs, tpd, nnb,
    rhs_hbm, psol_hbm, panel_hbm, win_hbm, dinv_hbm, tlist_hbm, nlist_hbm, force_hbm,
    sol_out, res_out,
    tlist, nlist, psol, panel, win, dinv, force, xpast, xx, whi, wlo, mhi, mlo, fhi, flo, acc,
    part, rs_buf, outp, usend, ubuf, vout, vbuf, y_all, rhs_all,
    load_sem, panel_sem, rhs_sem,
    rs_send, rs_recv, df_send, df_recv, dx_send, ch_send, sc_send, ln_send, ag_send, y_recv,
    rl_send, ra_send, r_recv, v_send, v_recv,
):
    p = lax.axis_index("prow")
    q = lax.axis_index("pcol")
    order = owners * tile
    owner = q < owners
    mine = lax.rem(q, owners)
    barrier = pltpu.get_barrier_semaphore()

    def at_plane(step):
        return lax.rem(q + 1 + step, cols)

    def at_line(step):
        return lax.rem(p + 1 + step, rows)

    def remote(src, dst, send, recv, row, col):
        return pltpu.make_async_remote_copy(
            src_ref=src, dst_ref=dst, send_sem=send, recv_sem=recv,
            device_id=(row, col), device_id_type=MESH,
        )

    def act(copy, go):
        if go:
            copy.start()
        else:
            copy.wait_send()

    first = pltpu.make_async_copy(psol_hbm, psol, load_sem.at[0])
    first.start()

    def panel_copy(c):
        at = pl.ds(pl.multiple_of(c * tile, tile), tile)
        return pltpu.make_async_copy(panel_hbm.at[at, :], panel.at[at, :], panel_sem.at[c])

    @pl.loop(0, owners)
    def _(i):
        panel_copy(i).start()

    def rhs_copy(c):
        return pltpu.make_async_copy(
            rhs_hbm.at[:, c * tile:(c + 1) * tile], rhs_all.at[p * owners + c], rhs_sem.at[c]
        )

    for c in range(owners):
        rhs_copy(c).start()
    load_dinv = pltpu.make_async_copy(dinv_hbm.at[0], dinv, load_sem.at[1])
    load_win = pltpu.make_async_copy(win_hbm.at[0, :, 0, :], win, load_sem.at[2])
    load_force = pltpu.make_async_copy(force_hbm.at[0], force, load_sem.at[3])
    load_tlist = pltpu.make_async_copy(tlist_hbm, tlist, load_sem.at[4])
    load_nlist = pltpu.make_async_copy(nlist_hbm, nlist, load_sem.at[5])

    @pl.when(q < p)
    def _():
        load_win.start()

    load_tlist.start()
    load_nlist.start()

    @pl.loop(0, cols - 1)
    def _(i):
        pl.semaphore_signal(barrier, inc=1, device_id=(p, at_plane(i)), device_id_type=MESH)

    @pl.loop(0, rows - 1)
    def _(i):
        pl.semaphore_signal(barrier, inc=1, device_id=(at_line(i), q), device_id_type=MESH)

    @pl.when((p >= 2) & (q == p - 1))
    def _():
        pl.semaphore_signal(barrier, inc=1, device_id=(p - 1, q - 1), device_id_type=MESH)

    @pl.when((p == 1) & (q == 0))
    def _():
        @pl.loop(1, owners)
        def _(c):
            pl.semaphore_signal(barrier, inc=1, device_id=(0, c), device_id_type=MESH)

    first.wait()
    for at in range(0, psol.shape[1], tile):
        xpast[at:at + tile, :] = turned(psol[:, at:at + tile])

    def rhs_line(go):
        t = p * owners + mine

        @pl.when(owner)
        def _():
            @pl.loop(0, rows - 1)
            def _(i):
                act(remote(rhs_all.at[t], rhs_all.at[t], rl_send.at[i], r_recv.at[t], at_line(i), q), go)

    def fold(value):
        turned = value.T
        return turned[:nrhs] + turned[nrhs:]

    def pack(ref, base):
        for c in range(owners):
            xx[c * tile:(c + 1) * tile, :] = turned(ref[base + c])

    def rs_copy(c):
        return remote(outp.at[c], rs_buf.at[q], rs_send.at[c], rs_recv.at[q], p, c)

    step = min(256, order)
    pair = step // tile

    @pl.loop(0, order // step)
    def _(i):
        for n in range(pair):
            panel_copy(i * pair + n).wait()

        @pl.when(i == max(order // step // 2 - 1, 0))
        def _():
            load_dinv.start()

        high, low = halves(panel[pl.ds(pl.multiple_of(i * step, step), step), :])
        weights = xpast[...]
        value = nn(high, weights) + nn(low, weights)
        for n in range(pair):
            part[i * pair + n] = fold(value[n * tile:(n + 1) * tile])

    load_force.start()
    for c in range(owners):
        rhs_copy(c).wait()
    passes_on = ((p == 0) & owner & (q > 0)) | ((p > 0) & (p < rows - 1) & (q == p - 1))
    pl.semaphore_wait(barrier, cols - 1 + rows - 1 + jnp.where(passes_on, 1, 0))

    rhs_line(True)

    @pl.when(q == 0)
    def _():
        for c in range(owners):
            part[c] = part[c] - rhs_all[p * owners + c]

    load_dinv.wait()
    pack(part, 0)
    for at in range(0, order, step):
        depth = at + step
        high, low = halves(dinv[at:depth, :depth])
        weights = xx[:depth, :]
        value = nn(high, weights) + nn(low, weights)
        for n in range(pair):
            c = at // tile + n
            outp[c] = fold(value[n * tile:(n + 1) * tile])

            @pl.when(c != q)
            def _():
                rs_copy(c).start()

    @pl.when(q < p)
    def _():
        load_win.wait()
        for at in range(0, order, step):
            high, low = halves(win[at:at + step, :])
            whi[at:at + step, :] = high
            wlo[at:at + step, :] = low
        for at in range(0, order, step):
            depth = at + step
            high, low = halves(dinv[at:at + step, :depth])
            value = nn(high, whi[:depth, :]) + nn(low, whi[:depth, :]) + nn(high, wlo[:depth, :])
            high, low = halves(value)
            mhi[at:at + step, :] = high
            mlo[at:at + step, :] = low

    solver = (p > 0) & (q == p - 1)

    def df_send_one(go):
        @pl.when(owner & (p > 0) & jnp.logical_not(solver))
        def _():
            act(remote(usend, ubuf.at[mine], df_send, df_recv.at[mine], p, p - 1), go)

    def first_send(go):
        @pl.when(owner & (p == 0))
        def _():
            act(remote(y_all.at[mine], y_all.at[mine], dx_send.at[mine], y_recv.at[mine], 1, 0), go)

    def line_send(k, go):
        t = k * owners + mine

        @pl.when(owner)
        def _():
            @pl.loop(0, rows - 1)
            def _(i):
                @pl.when((q != k) | (at_line(i) < k))
                def _():
                    act(remote(y_all.at[t], y_all.at[t], ln_send.at[i], y_recv.at[t], at_line(i), q), go)

    def has_whole(k, row, col):
        handed = (row > k) & (col == k)
        return handed if k == 0 else handed | ((row == k) & (col == k - 1))

    def plane_send(k, go):
        t = k * owners + mine

        @pl.when(owner)
        def _():
            @pl.loop(0, cols - 1)
            def _(i):
                d = at_plane(i)

                @pl.when(jnp.logical_not(has_whole(k, p, d)))
                def _():
                    act(remote(y_all.at[t], y_all.at[t], ag_send.at[k, i], y_recv.at[t], p, d), go)

    def solved_send(k, c, go):
        t = k * owners + c
        if k < rows - 1:
            act(remote(y_all.at[t], y_all.at[t], dx_send.at[c], y_recv.at[t], p + 1, k), go)

        @pl.when(c != q)
        def _():
            act(remote(y_all.at[t], y_all.at[t], sc_send.at[c], y_recv.at[t], p, c), go)

    def chain_send(k, c, go):
        t = k * owners + c

        @pl.when(p < rows - 1)
        def _():
            act(remote(y_all.at[t], y_all.at[t], ch_send.at[c], y_recv.at[t], p + 1, q), go)

    def v_send_one(j, c, go):
        act(remote(vout.at[c], vbuf.at[j, c], v_send.at[c], v_recv.at[j, c], p, p - 1), go)

    def y_wait(t):
        remote(y_all.at[t], y_all.at[t], ln_send.at[0], y_recv.at[t], p, at_plane(0)).wait_recv()

    def rhs_plane(go):
        @pl.when(owner)
        def _():
            @pl.loop(0, rows - 1)
            def _(j):
                t = at_line(j) * owners + mine
                if go:
                    remote(rhs_all.at[t], rhs_all.at[t], rl_send.at[0], r_recv.at[t], p, at_plane(0)).wait_recv()

                @pl.loop(0, cols - 1)
                def _(i):
                    act(remote(rhs_all.at[t], rhs_all.at[t], ra_send.at[j, i], r_recv.at[t], p, at_plane(i)), go)

    @pl.when(owner)
    def _():
        @pl.loop(0, cols - 1)
        def _(i):
            s = at_plane(i)
            remote(outp.at[mine], rs_buf.at[s], rs_send.at[mine], rs_recv.at[s], p, s).wait_recv()

        total = outp[mine]
        for i in range(cols - 1):
            total = total + rs_buf[at_plane(i)]

        @pl.when(p == 0)
        def _():
            y_all[mine] = -total

        @pl.when(solver)
        def _():
            ubuf[mine] = -total

        @pl.when((p > 0) & jnp.logical_not(solver))
        def _():
            usend[...] = -total

    first_send(True)
    df_send_one(True)

    @pl.when(p >= 2)
    def _():
        rhs_plane(True)

    @pl.when(solver)
    def _():
        for c in range(owners):
            @pl.when(c != q)
            def _():
                remote(usend, ubuf.at[c], df_send, df_recv.at[c], p, at_plane(0)).wait_recv()

    for k in range(rows):
        base = k * owners
        handed = (p > k) & (q == k)
        made = p == k if k == 0 else (p == k) & (q == k - 1)

        @pl.when(handed)
        def _():
            last = order - step
            for at in range(0, order, step):
                for n in range(pair):
                    c = at // tile + n
                    y_wait(base + c)
                    chain_send(k, c, True)
                    xx[c * tile:(c + 1) * tile, :] = turned(y_all[base + c])
                if at < last:
                    weights = xx[at:at + step, :]
                    value = nn(mhi[:, at:at + step], weights) + nn(mlo[:, at:at + step], weights)
                    acc[...] = value if at == 0 else acc[...] + value

            def product(at):
                weights = xx[last:, :]
                value = nn(mhi[at:at + step, last:], weights) + nn(mlo[at:at + step, last:], weights)
                return acc[at:at + step, :] + value

            @pl.when(p == k + 1)
            def _():
                for j in range(k):
                    @pl.loop(0, owners)
                    def _(c):
                        remote(vout.at[c], vbuf.at[j, c], v_send.at[c], v_recv.at[j, c], p, at_plane(0)).wait_recv()

                for at in range(0, order, step):
                    whole = product(at)
                    for n in range(pair):
                        c = at // tile + n
                        value = ubuf[c] - fold(whole[n * tile:(n + 1) * tile])
                        for j in range(k):
                            value = value - vbuf[j, c]
                        y_all[base + owners + c] = value
                        if k < rows - 1:
                            solved_send(k + 1, c, True)

            @pl.when(p > k + 1)
            def _():
                for at in range(0, order, step):
                    whole = product(at)
                    for n in range(pair):
                        c = at // tile + n
                        vout[c] = fold(whole[n * tile:(n + 1) * tile])
                        v_send_one(k, c, True)

        @pl.when(owner & jnp.logical_not(made | handed))
        def _():
            y_wait(base + mine)

        @pl.when(p == k)
        def _():
            line_send(k, True)

        plane_send(k, True)

        @pl.when((p == k) & (p < 2))
        def _():
            rhs_plane(True)

    load_force.wait()
    for t in range(tpd):
        for n in range(nnb):
            high, low = halves(force[t, n])
            fhi[t, :, n * tile:(n + 1) * tile] = high
            flo[t, :, n * tile:(n + 1) * tile] = low

    for k in range(rows):
        @pl.when(jnp.logical_not(has_whole(k, p, q)))
        def _():
            @pl.loop(0, cols - 1)
            def _(i):
                c = at_plane(i)

                @pl.when(c < owners)
                def _():
                    y_wait(k * owners + c)

    for c in range(owners):
        sol_out[:, c * tile:(c + 1) * tile] = y_all[p * owners + c]

    load_tlist.wait()
    load_nlist.wait()

    @pl.loop(0, rows - 1)
    def _(j):
        @pl.loop(0, cols - 1)
        def _(i):
            c = at_plane(i)

            @pl.when(c < owners)
            def _():
                t = at_line(j) * owners + c
                remote(rhs_all.at[t], rhs_all.at[t], rl_send.at[0], r_recv.at[t], p, at_plane(0)).wait_recv()

    for t in range(tpd):
        weights = jnp.concatenate([turned(y_all[nlist[0, t, n]]) for n in range(nnb)], axis=0)
        term = fold(nn(fhi[t], weights) + nn(flo[t], weights))
        res_out[0, t] = rhs_all[tlist[0, t]] - term

    rhs_line(False)

    @pl.loop(0, owners)
    def _(c):
        @pl.when(c != q)
        def _():
            rs_copy(c).wait_send()

    first_send(False)
    df_send_one(False)
    rhs_plane(False)
    for k in range(rows):
        @pl.when(p == k)
        def _():
            line_send(k, False)

        if k > 0:
            @pl.when((p == k) & (q == k - 1))
            def _():
                @pl.loop(0, owners)
                def _(c):
                    solved_send(k, c, False)

        @pl.when((p > k) & (q == k))
        def _():
            @pl.loop(0, owners)
            def _(c):
                chain_send(k, c, False)

                @pl.when(p > k + 1)
                def _():
                    v_send_one(k, c, False)

        plane_send(k, False)


def per_device(rows, cols, window_rhs, past_solution, past_panel, window_panel, diag_inverse, tile_list, neighbor_list, force_constants):
    nrhs, order = window_rhs.shape
    depth = past_solution.shape[1]
    tpd, nnb, tile = force_constants.shape[1:4]
    owners = order // tile
    tiles = rows * owners
    hbm = pl.BlockSpec(memory_space=pltpu.HBM)
    vmem = pl.BlockSpec(memory_space=pltpu.VMEM)
    dma = pltpu.SemaphoreType.DMA
    return pl.pallas_call(
        functools.partial(kernel, rows, cols, owners, tile, nrhs, tpd, nnb),
        out_shape=(
            jax.ShapeDtypeStruct((nrhs, order), F32),
            jax.ShapeDtypeStruct((1, tpd, nrhs, tile), F32),
        ),
        in_specs=[hbm] * 8,
        out_specs=(vmem, vmem),
        scratch_shapes=[
            pltpu.SMEM((1, tpd), jnp.int32),
            pltpu.SMEM((1, tpd, nnb), jnp.int32),
            pltpu.VMEM((nrhs, depth), F32),
            pltpu.VMEM((order, depth), F32),
            pltpu.VMEM((order, order), F32),
            pltpu.VMEM((order, order), F32),
            pltpu.VMEM((tpd, nnb, tile, tile), F32),
            pltpu.VMEM((depth, 2 * nrhs), BF16),
            pltpu.VMEM((order, 2 * nrhs), BF16),
            pltpu.VMEM((order, order), BF16),
            pltpu.VMEM((order, order), BF16),
            pltpu.VMEM((order, order), BF16),
            pltpu.VMEM((order, order), BF16),
            pltpu.VMEM((tpd, tile, nnb * tile), BF16),
            pltpu.VMEM((tpd, tile, nnb * tile), BF16),
            pltpu.VMEM((order, 2 * nrhs), F32),
            pltpu.VMEM((owners, nrhs, tile), F32),
            pltpu.VMEM((cols, nrhs, tile), F32),
            pltpu.VMEM((owners, nrhs, tile), F32),
            pltpu.VMEM((nrhs, tile), F32),
            pltpu.VMEM((owners, nrhs, tile), F32),
            pltpu.VMEM((owners, nrhs, tile), F32),
            pltpu.VMEM((max(rows - 2, 1), owners, nrhs, tile), F32),
            pltpu.VMEM((tiles, nrhs, tile), F32),
            pltpu.VMEM((tiles, nrhs, tile), F32),
            dma((6,)),
            dma((owners,)),
            dma((owners,)),
            dma((owners,)),
            dma((cols,)),
            dma,
            dma((owners,)),
            dma((owners,)),
            dma((owners,)),
            dma((owners,)),
            dma((rows,)),
            dma((rows, cols)),
            dma((tiles,)),
            dma((rows,)),
            dma((rows, cols)),
            dma((tiles,)),
            dma((owners,)),
            dma((rows, owners)),
        ],
        compiler_params=pltpu.CompilerParams(
            collective_id=0, has_side_effects=True, vmem_limit_bytes=63 * 2**20
        ),
    )(window_rhs, past_solution, past_panel, window_panel, diag_inverse, tile_list, neighbor_list, force_constants)


def solution(mesh):
    placed = (
        P(None, "prow"),
        P(None, "pcol"),
        P("prow", "pcol"),
        P("prow", None, "pcol", None),
        P("prow", None, None),
        P(("prow", "pcol"), None),
        P(("prow", "pcol"), None, None),
        P(("prow", "pcol"), None, None, None, None),
    )
    return jax.shard_map(
        functools.partial(per_device, mesh.shape["prow"], mesh.shape["pcol"]),
        mesh=mesh,
        in_specs=placed,
        out_specs=(P(None, "prow"), P(("prow", "pcol"), None, None, None)),
        check_vma=False,
    )
```

```python
import functools

import jax
import jax.numpy as jnp
from jax import lax
from jax.experimental import pallas as pl
from jax.experimental.pallas import tpu as pltpu
from jax.sharding import PartitionSpec as P

MESH = pl.DeviceIdType.MESH
BF16 = jnp.bfloat16
F32 = jnp.float32


def halves(value):
    high = value.astype(BF16)
    return high, (value - high.astype(F32)).astype(BF16)


def nn(left, right):
    return lax.dot_general(left, right, (((1,), (0,)), ((), ())), preferred_element_type=F32)


def turned(block):
    high = block.astype(BF16).astype(F32)
    return jnp.concatenate([high, block - high], axis=0).T.astype(BF16)


def kernel(
    rows, cols, owners, tile, nrhs, tpd, nnb,
    rhs_hbm, psol_hbm, panel_hbm, win_hbm, dinv_hbm, tlist_hbm, nlist_hbm, force_hbm,
    sol_out, res_out,
    tlist, nlist, psol, panel, win, dinv, force, xpast, xx, whi, wlo, mhi, mlo, fhi, flo, acc,
    part, rs_buf, outp, usend, ubuf, vout, vbuf, y_all, rhs_all,
    load_sem, panel_sem, rhs_sem,
    rs_send, rs_recv, df_send, df_recv, dx_send, ch_send, sc_send, ln_send, ag_send, y_recv,
    rl_send, ra_send, r_recv, v_send, v_recv,
):
    p = lax.axis_index("prow")
    q = lax.axis_index("pcol")
    order = owners * tile
    owner = q < owners
    mine = lax.rem(q, owners)
    barrier = pltpu.get_barrier_semaphore()

    def at_plane(step):
        return lax.rem(q + 1 + step, cols)

    def at_line(step):
        return lax.rem(p + 1 + step, rows)

    def remote(src, dst, send, recv, row, col):
        return pltpu.make_async_remote_copy(
            src_ref=src, dst_ref=dst, send_sem=send, recv_sem=recv,
            device_id=(row, col), device_id_type=MESH,
        )

    def act(copy, go):
        if go:
            copy.start()
        else:
            copy.wait_send()

    first = pltpu.make_async_copy(psol_hbm, psol, load_sem.at[0])
    first.start()

    def panel_copy(c):
        at = pl.ds(pl.multiple_of(c * tile, tile), tile)
        return pltpu.make_async_copy(panel_hbm.at[at, :], panel.at[at, :], panel_sem.at[c])

    @pl.loop(0, owners)
    def _(i):
        panel_copy(i).start()

    def rhs_copy(c):
        return pltpu.make_async_copy(
            rhs_hbm.at[:, c * tile:(c + 1) * tile], rhs_all.at[p * owners + c], rhs_sem.at[c]
        )

    for c in range(owners):
        rhs_copy(c).start()
    load_dinv = pltpu.make_async_copy(dinv_hbm.at[0], dinv, load_sem.at[1])
    load_win = pltpu.make_async_copy(win_hbm.at[0, :, 0, :], win, load_sem.at[2])
    load_force = pltpu.make_async_copy(force_hbm.at[0], force, load_sem.at[3])
    load_tlist = pltpu.make_async_copy(tlist_hbm, tlist, load_sem.at[4])
    load_nlist = pltpu.make_async_copy(nlist_hbm, nlist, load_sem.at[5])

    @pl.when(q < p)
    def _():
        load_win.start()

    load_tlist.start()
    load_nlist.start()

    @pl.loop(0, cols - 1)
    def _(i):
        pl.semaphore_signal(barrier, inc=1, device_id=(p, at_plane(i)), device_id_type=MESH)

    @pl.loop(0, rows - 1)
    def _(i):
        pl.semaphore_signal(barrier, inc=1, device_id=(at_line(i), q), device_id_type=MESH)

    @pl.when((p >= 2) & (q == p - 1))
    def _():
        pl.semaphore_signal(barrier, inc=1, device_id=(p - 1, q - 1), device_id_type=MESH)

    @pl.when((p == 1) & (q == 0))
    def _():
        @pl.loop(1, owners)
        def _(c):
            pl.semaphore_signal(barrier, inc=1, device_id=(0, c), device_id_type=MESH)

    first.wait()
    for at in range(0, psol.shape[1], tile):
        xpast[at:at + tile, :] = turned(psol[:, at:at + tile])

    def rhs_line(go):
        t = p * owners + mine

        @pl.when(owner)
        def _():
            @pl.loop(0, rows - 1)
            def _(i):
                act(remote(rhs_all.at[t], rhs_all.at[t], rl_send.at[i], r_recv.at[t], at_line(i), q), go)

    def fold(value):
        turned = value.T
        return turned[:nrhs] + turned[nrhs:]

    def pack(ref, base):
        for c in range(owners):
            xx[c * tile:(c + 1) * tile, :] = turned(ref[base + c])

    def rs_copy(c):
        return remote(outp.at[c], rs_buf.at[q], rs_send.at[c], rs_recv.at[q], p, c)

    step = min(256, order)
    pair = step // tile

    @pl.loop(0, order // step)
    def _(i):
        for n in range(pair):
            panel_copy(i * pair + n).wait()

        @pl.when(i == max(order // step // 2 - 1, 0))
        def _():
            load_dinv.start()

        high, low = halves(panel[pl.ds(pl.multiple_of(i * step, step), step), :])
        weights = xpast[...]
        value = nn(high, weights) + nn(low, weights)
        for n in range(pair):
            part[i * pair + n] = fold(value[n * tile:(n + 1) * tile])

    load_force.start()
    for c in range(owners):
        rhs_copy(c).wait()
    passes_on = ((p == 0) & owner & (q > 0)) | ((p > 0) & (p < rows - 1) & (q == p - 1))
    pl.semaphore_wait(barrier, cols - 1 + rows - 1 + jnp.where(passes_on, 1, 0))

    rhs_line(True)

    @pl.when(q == 0)
    def _():
        for c in range(owners):
            part[c] = part[c] - rhs_all[p * owners + c]

    load_dinv.wait()
    pack(part, 0)
    for at in range(0, order, step):
        depth = at + step
        high, low = halves(dinv[at:depth, :depth])
        weights = xx[:depth, :]
        value = nn(high, weights) + nn(low, weights)
        for n in range(pair):
            c = at // tile + n
            outp[c] = fold(value[n * tile:(n + 1) * tile])

            @pl.when(c != q)
            def _():
                rs_copy(c).start()

    @pl.when((p == 1) & (q == 0))
    def _():
        load_win.wait()
        for at in range(0, order, step):
            high, low = halves(win[at:at + step, :])
            mhi[at:at + step, :] = high
            mlo[at:at + step, :] = low
            high, low = halves(dinv[at:at + step, :])
            whi[at:at + step, :] = high
            wlo[at:at + step, :] = low

    @pl.when((q < p) & (p > 1))
    def _():
        load_win.wait()
        for at in range(0, order, step):
            high, low = halves(win[at:at + step, :])
            whi[at:at + step, :] = high
            wlo[at:at + step, :] = low
        for at in range(0, order, step):
            depth = at + step
            high, low = halves(dinv[at:at + step, :depth])
            value = nn(high, whi[:depth, :]) + nn(low, whi[:depth, :]) + nn(high, wlo[:depth, :])
            high, low = halves(value)
            mhi[at:at + step, :] = high
            mlo[at:at + step, :] = low

    solver = (p > 0) & (q == p - 1)

    def df_send_one(go):
        @pl.when(owner & (p > 0) & jnp.logical_not(solver))
        def _():
            act(remote(usend, ubuf.at[mine], df_send, df_recv.at[mine], p, p - 1), go)

    def first_send(go):
        @pl.when(owner & (p == 0))
        def _():
            act(remote(y_all.at[mine], y_all.at[mine], dx_send.at[mine], y_recv.at[mine], 1, 0), go)

    def line_send(k, go):
        t = k * owners + mine

        @pl.when(owner)
        def _():
            @pl.loop(0, rows - 1)
            def _(i):
                @pl.when((q != k) | (at_line(i) < k))
                def _():
                    act(remote(y_all.at[t], y_all.at[t], ln_send.at[i], y_recv.at[t], at_line(i), q), go)

    def has_whole(k, row, col):
        handed = (row > k) & (col == k)
        return handed if k == 0 else handed | ((row == k) & (col == k - 1))

    def plane_send(k, go):
        t = k * owners + mine

        @pl.when(owner)
        def _():
            @pl.loop(0, cols - 1)
            def _(i):
                d = at_plane(i)

                @pl.when(jnp.logical_not(has_whole(k, p, d)))
                def _():
                    act(remote(y_all.at[t], y_all.at[t], ag_send.at[k, i], y_recv.at[t], p, d), go)

    def solved_send(k, c, go):
        t = k * owners + c
        if k < rows - 1:
            act(remote(y_all.at[t], y_all.at[t], dx_send.at[c], y_recv.at[t], p + 1, k), go)

        @pl.when(c != q)
        def _():
            act(remote(y_all.at[t], y_all.at[t], sc_send.at[c], y_recv.at[t], p, c), go)

    def chain_send(k, c, go):
        t = k * owners + c

        @pl.when(p < rows - 1)
        def _():
            act(remote(y_all.at[t], y_all.at[t], ch_send.at[c], y_recv.at[t], p + 1, q), go)

    def v_send_one(j, c, go):
        act(remote(vout.at[c], vbuf.at[j, c], v_send.at[c], v_recv.at[j, c], p, p - 1), go)

    def y_wait(t):
        remote(y_all.at[t], y_all.at[t], ln_send.at[0], y_recv.at[t], p, at_plane(0)).wait_recv()

    def rhs_plane(go):
        @pl.when(owner)
        def _():
            @pl.loop(0, rows - 1)
            def _(j):
                t = at_line(j) * owners + mine
                if go:
                    remote(rhs_all.at[t], rhs_all.at[t], rl_send.at[0], r_recv.at[t], p, at_plane(0)).wait_recv()

                @pl.loop(0, cols - 1)
                def _(i):
                    act(remote(rhs_all.at[t], rhs_all.at[t], ra_send.at[j, i], r_recv.at[t], p, at_plane(i)), go)

    @pl.when(owner)
    def _():
        @pl.loop(0, cols - 1)
        def _(i):
            s = at_plane(i)
            remote(outp.at[mine], rs_buf.at[s], rs_send.at[mine], rs_recv.at[s], p, s).wait_recv()

        total = outp[mine]
        for i in range(cols - 1):
            total = total + rs_buf[at_plane(i)]

        @pl.when(p == 0)
        def _():
            y_all[mine] = -total

        @pl.when(solver)
        def _():
            ubuf[mine] = -total

        @pl.when((p > 0) & jnp.logical_not(solver))
        def _():
            usend[...] = -total

    first_send(True)
    df_send_one(True)

    @pl.when(p >= 2)
    def _():
        rhs_plane(True)

    @pl.when(solver)
    def _():
        for c in range(owners):
            @pl.when(c != q)
            def _():
                remote(usend, ubuf.at[c], df_send, df_recv.at[c], p, at_plane(0)).wait_recv()

    for k in range(rows):
        base = k * owners
        handed = (p > k) & (q == k)
        made = p == k if k == 0 else (p == k) & (q == k - 1)

        @pl.when(handed)
        def _():
            last = order - step
            for at in range(0, order, step):
                for n in range(pair):
                    c = at // tile + n
                    y_wait(base + c)
                    chain_send(k, c, True)
                    xx[c * tile:(c + 1) * tile, :] = turned(y_all[base + c])
                if at < last:
                    weights = xx[at:at + step, :]
                    value = nn(mhi[:, at:at + step], weights) + nn(mlo[:, at:at + step], weights)
                    acc[...] = value if at == 0 else acc[...] + value

            def product(at):
                weights = xx[last:, :]
                value = nn(mhi[at:at + step, last:], weights) + nn(mlo[at:at + step, last:], weights)
                return acc[at:at + step, :] + value

            @pl.when(p == k + 1)
            def _():
                for j in range(k):
                    @pl.loop(0, owners)
                    def _(c):
                        remote(vout.at[c], vbuf.at[j, c], v_send.at[c], v_recv.at[j, c], p, at_plane(0)).wait_recv()

                if k == 0:
                    for at in range(0, order, step):
                        whole = product(at)
                        for n in range(pair):
                            part[at // tile + n] = fold(whole[n * tile:(n + 1) * tile])
                    pack(part, 0)

                for at in range(0, order, step):
                    if k == 0:
                        weights = xx[:at + step, :]
                        whole = nn(whi[at:at + step, :at + step], weights) + nn(wlo[at:at + step, :at + step], weights)
                    else:
                        whole = product(at)
                    for n in range(pair):
                        c = at // tile + n
                        value = ubuf[c] - fold(whole[n * tile:(n + 1) * tile])
                        for j in range(k):
                            value = value - vbuf[j, c]
                        y_all[base + owners + c] = value
                        if k < rows - 1:
                            solved_send(k + 1, c, True)

            @pl.when(p > k + 1)
            def _():
                for at in range(0, order, step):
                    whole = product(at)
                    for n in range(pair):
                        c = at // tile + n
                        vout[c] = fold(whole[n * tile:(n + 1) * tile])
                        v_send_one(k, c, True)

        @pl.when(owner & jnp.logical_not(made | handed))
        def _():
            y_wait(base + mine)

        @pl.when(p == k)
        def _():
            line_send(k, True)

        plane_send(k, True)

        @pl.when((p == k) & (p < 2))
        def _():
            rhs_plane(True)

    load_force.wait()
    for t in range(tpd):
        for n in range(nnb):
            high, low = halves(force[t, n])
            fhi[t, :, n * tile:(n + 1) * tile] = high
            flo[t, :, n * tile:(n + 1) * tile] = low

    for k in range(rows):
        @pl.when(jnp.logical_not(has_whole(k, p, q)))
        def _():
            @pl.loop(0, cols - 1)
            def _(i):
                c = at_plane(i)

                @pl.when(c < owners)
                def _():
                    y_wait(k * owners + c)

    for c in range(owners):
        sol_out[:, c * tile:(c + 1) * tile] = y_all[p * owners + c]

    load_tlist.wait()
    load_nlist.wait()

    @pl.loop(0, rows - 1)
    def _(j):
        @pl.loop(0, cols - 1)
        def _(i):
            c = at_plane(i)

            @pl.when(c < owners)
            def _():
                t = at_line(j) * owners + c
                remote(rhs_all.at[t], rhs_all.at[t], rl_send.at[0], r_recv.at[t], p, at_plane(0)).wait_recv()

    for t in range(tpd):
        weights = jnp.concatenate([turned(y_all[nlist[0, t, n]]) for n in range(nnb)], axis=0)
        term = fold(nn(fhi[t], weights) + nn(flo[t], weights))
        res_out[0, t] = rhs_all[tlist[0, t]] - term

    rhs_line(False)

    @pl.loop(0, owners)
    def _(c):
        @pl.when(c != q)
        def _():
            rs_copy(c).wait_send()

    first_send(False)
    df_send_one(False)
    rhs_plane(False)
    for k in range(rows):
        @pl.when(p == k)
        def _():
            line_send(k, False)

        if k > 0:
            @pl.when((p == k) & (q == k - 1))
            def _():
                @pl.loop(0, owners)
                def _(c):
                    solved_send(k, c, False)

        @pl.when((p > k) & (q == k))
        def _():
            @pl.loop(0, owners)
            def _(c):
                chain_send(k, c, False)

                @pl.when(p > k + 1)
                def _():
                    v_send_one(k, c, False)

        plane_send(k, False)


def per_device(rows, cols, window_rhs, past_solution, past_panel, window_panel, diag_inverse, tile_list, neighbor_list, force_constants):
    nrhs, order = window_rhs.shape
    depth = past_solution.shape[1]
    tpd, nnb, tile = force_constants.shape[1:4]
    owners = order // tile
    tiles = rows * owners
    hbm = pl.BlockSpec(memory_space=pltpu.HBM)
    vmem = pl.BlockSpec(memory_space=pltpu.VMEM)
    dma = pltpu.SemaphoreType.DMA
    return pl.pallas_call(
        functools.partial(kernel, rows, cols, owners, tile, nrhs, tpd, nnb),
        out_shape=(
            jax.ShapeDtypeStruct((nrhs, order), F32),
            jax.ShapeDtypeStruct((1, tpd, nrhs, tile), F32),
        ),
        in_specs=[hbm] * 8,
        out_specs=(vmem, vmem),
        scratch_shapes=[
            pltpu.SMEM((1, tpd), jnp.int32),
            pltpu.SMEM((1, tpd, nnb), jnp.int32),
            pltpu.VMEM((nrhs, depth), F32),
            pltpu.VMEM((order, depth), F32),
            pltpu.VMEM((order, order), F32),
            pltpu.VMEM((order, order), F32),
            pltpu.VMEM((tpd, nnb, tile, tile), F32),
            pltpu.VMEM((depth, 2 * nrhs), BF16),
            pltpu.VMEM((order, 2 * nrhs), BF16),
            pltpu.VMEM((order, order), BF16),
            pltpu.VMEM((order, order), BF16),
            pltpu.VMEM((order, order), BF16),
            pltpu.VMEM((order, order), BF16),
            pltpu.VMEM((tpd, tile, nnb * tile), BF16),
            pltpu.VMEM((tpd, tile, nnb * tile), BF16),
            pltpu.VMEM((order, 2 * nrhs), F32),
            pltpu.VMEM((owners, nrhs, tile), F32),
            pltpu.VMEM((cols, nrhs, tile), F32),
            pltpu.VMEM((owners, nrhs, tile), F32),
            pltpu.VMEM((nrhs, tile), F32),
            pltpu.VMEM((owners, nrhs, tile), F32),
            pltpu.VMEM((owners, nrhs, tile), F32),
            pltpu.VMEM((max(rows - 2, 1), owners, nrhs, tile), F32),
            pltpu.VMEM((tiles, nrhs, tile), F32),
            pltpu.VMEM((tiles, nrhs, tile), F32),
            dma((6,)),
            dma((owners,)),
            dma((owners,)),
            dma((owners,)),
            dma((cols,)),
            dma,
            dma((owners,)),
            dma((owners,)),
            dma((owners,)),
            dma((owners,)),
            dma((rows,)),
            dma((rows, cols)),
            dma((tiles,)),
            dma((rows,)),
            dma((rows, cols)),
            dma((tiles,)),
            dma((owners,)),
            dma((rows, owners)),
        ],
        compiler_params=pltpu.CompilerParams(
            collective_id=0, has_side_effects=True, vmem_limit_bytes=63 * 2**20
        ),
    )(window_rhs, past_solution, past_panel, window_panel, diag_inverse, tile_list, neighbor_list, force_constants)


def solution(mesh):
    placed = (
        P(None, "prow"),
        P(None, "pcol"),
        P("prow", "pcol"),
        P("prow", None, "pcol", None),
        P("prow", None, None),
        P(("prow", "pcol"), None),
        P(("prow", "pcol"), None, None),
        P(("prow", "pcol"), None, None, None, None),
    )
    return jax.shard_map(
        functools.partial(per_device, mesh.shape["prow"], mesh.shape["pcol"]),
        mesh=mesh,
        in_specs=placed,
        out_specs=(P(None, "prow"), P(("prow", "pcol"), None, None, None)),
        check_vma=False,
    )
```

```python
import functools

import jax
import jax.numpy as jnp
from jax import lax
from jax.experimental import pallas as pl
from jax.experimental.pallas import tpu as pltpu
from jax.sharding import PartitionSpec as P

MESH = pl.DeviceIdType.MESH
BF16 = jnp.bfloat16
F32 = jnp.float32


def halves(value):
    high = value.astype(BF16)
    return high, (value - high.astype(F32)).astype(BF16)


def nn(left, right):
    return lax.dot_general(left, right, (((1,), (0,)), ((), ())), preferred_element_type=F32)


def turned(block):
    high = block.astype(BF16).astype(F32)
    return jnp.concatenate([high, block - high], axis=0).T.astype(BF16)


def kernel(
    rows, cols, owners, tile, nrhs, tpd, nnb,
    rhs_hbm, psol_hbm, panel_hbm, win_hbm, dinv_hbm, tlist_hbm, nlist_hbm, force_hbm,
    sol_out, res_out,
    tlist, nlist, psol, panel, win, dinv, force, xpast, xx, whi, wlo, mhi, mlo, fhi, flo, acc,
    part, rs_buf, outp, usend, ubuf, vout, vbuf, y_all, rhs_all,
    load_sem, panel_sem, rhs_sem,
    rs_send, rs_recv, df_send, df_recv, dx_send, ch_send, sc_send, ln_send, ag_send, y_recv,
    rl_send, ra_send, r_recv, v_send, v_recv,
):
    p = lax.axis_index("prow")
    q = lax.axis_index("pcol")
    order = owners * tile
    owner = q < owners
    mine = lax.rem(q, owners)
    barrier = pltpu.get_barrier_semaphore()

    def at_plane(step):
        return lax.rem(q + 1 + step, cols)

    def at_line(step):
        return lax.rem(p + 1 + step, rows)

    def remote(src, dst, send, recv, row, col):
        return pltpu.make_async_remote_copy(
            src_ref=src, dst_ref=dst, send_sem=send, recv_sem=recv,
            device_id=(row, col), device_id_type=MESH,
        )

    def act(copy, go):
        if go:
            copy.start()
        else:
            copy.wait_send()

    def piece(i, size):
        return pl.ds(pl.multiple_of(i * size, size), size)

    first = pltpu.make_async_copy(psol_hbm, psol, load_sem.at[0])
    first.start()

    def panel_copy(c):
        at = pl.ds(pl.multiple_of(c * tile, tile), tile)
        return pltpu.make_async_copy(panel_hbm.at[at, :], panel.at[at, :], panel_sem.at[c])

    @pl.loop(0, owners)
    def _(i):
        panel_copy(i).start()

    def rhs_copy(c):
        return pltpu.make_async_copy(
            rhs_hbm.at[:, c * tile:(c + 1) * tile], rhs_all.at[p * owners + c], rhs_sem.at[c]
        )

    for c in range(owners):
        rhs_copy(c).start()
    load_dinv = pltpu.make_async_copy(dinv_hbm.at[0], dinv, load_sem.at[1])
    load_win = pltpu.make_async_copy(win_hbm.at[0, :, 0, :], win, load_sem.at[2])
    load_force = pltpu.make_async_copy(force_hbm.at[0], force, load_sem.at[3])
    load_tlist = pltpu.make_async_copy(tlist_hbm, tlist, load_sem.at[4])
    load_nlist = pltpu.make_async_copy(nlist_hbm, nlist, load_sem.at[5])

    @pl.when(q < p)
    def _():
        load_win.start()

    load_tlist.start()
    load_nlist.start()

    @pl.loop(0, cols - 1)
    def _(i):
        pl.semaphore_signal(barrier, inc=1, device_id=(p, at_plane(i)), device_id_type=MESH)

    @pl.loop(0, rows - 1)
    def _(i):
        pl.semaphore_signal(barrier, inc=1, device_id=(at_line(i), q), device_id_type=MESH)

    @pl.when((p >= 2) & (q == p - 1))
    def _():
        pl.semaphore_signal(barrier, inc=1, device_id=(p - 1, q - 1), device_id_type=MESH)

    @pl.when((p == 1) & (q == 0))
    def _():
        @pl.loop(1, owners)
        def _(c):
            pl.semaphore_signal(barrier, inc=1, device_id=(0, c), device_id_type=MESH)

    first.wait()
    @pl.loop(0, psol.shape[1] // tile)
    def _(i):
        at = piece(i, tile)
        xpast[at, :] = turned(psol[:, at])


    def rhs_line(go):
        t = p * owners + mine

        @pl.when(owner)
        def _():
            @pl.loop(0, rows - 1)
            def _(i):
                act(remote(rhs_all.at[t], rhs_all.at[t], rl_send.at[i], r_recv.at[t], at_line(i), q), go)

    def fold(value):
        turned = value.T
        return turned[:nrhs] + turned[nrhs:]

    def pack(ref, base):
        @pl.loop(0, owners)
        def _(c):
            xx[piece(c, tile), :] = turned(ref[base + c])

    def rs_copy(c):
        return remote(outp.at[c], rs_buf.at[q], rs_send.at[c], rs_recv.at[q], p, c)

    step = min(256, order)
    pair = step // tile

    @pl.loop(0, order // step)
    def _(i):
        for n in range(pair):
            panel_copy(i * pair + n).wait()

        @pl.when(i == max(order // step // 2 - 1, 0))
        def _():
            load_dinv.start()

        high, low = halves(panel[pl.ds(pl.multiple_of(i * step, step), step), :])
        weights = xpast[...]
        value = nn(high, weights) + nn(low, weights)
        for n in range(pair):
            part[i * pair + n] = fold(value[n * tile:(n + 1) * tile])

    load_force.start()
    for c in range(owners):
        rhs_copy(c).wait()
    passes_on = ((p == 0) & owner & (q > 0)) | ((p > 0) & (p < rows - 1) & (q == p - 1))
    pl.semaphore_wait(barrier, cols - 1 + rows - 1 + jnp.where(passes_on, 1, 0))

    rhs_line(True)

    @pl.when(q == 0)
    def _():
        for c in range(owners):
            part[c] = part[c] - rhs_all[p * owners + c]

    load_dinv.wait()
    pack(part, 0)
    blocks = order // step

    @pl.loop(0, blocks)
    def _(i):
        def add(j, value):
            high, low = halves(dinv[piece(i, step), piece(j, step)])
            weights = xx[piece(j, step), :]
            return value + nn(high, weights) + nn(low, weights)

        value = lax.fori_loop(0, i + 1, add, jnp.zeros((step, 2 * nrhs), F32))
        for n in range(pair):
            c = i * pair + n
            outp[c] = fold(value[n * tile:(n + 1) * tile])

            @pl.when(c != q)
            def _():
                rs_copy(c).start()

    @pl.when(q < p)
    def _():
        load_win.wait()
        @pl.loop(0, blocks)
        def _(i):
            high, low = halves(win[piece(i, step), :])
            whi[piece(i, step), :] = high
            wlo[piece(i, step), :] = low

        @pl.loop(0, blocks)
        def _(i):
            at = piece(i, step)

            def add(j, value):
                high, low = halves(dinv[at, piece(j, step)])
                left = whi[piece(j, step), :]
                return value + nn(high, left) + nn(low, left) + nn(high, wlo[piece(j, step), :])

            value = lax.fori_loop(0, i + 1, add, jnp.zeros((step, order), F32))
            high, low = halves(value)
            mhi[at, :] = high
            mlo[at, :] = low

    solver = (p > 0) & (q == p - 1)

    def df_send_one(go):
        @pl.when(owner & (p > 0) & jnp.logical_not(solver))
        def _():
            act(remote(usend, ubuf.at[mine], df_send, df_recv.at[mine], p, p - 1), go)

    def first_send(go):
        @pl.when(owner & (p == 0))
        def _():
            act(remote(y_all.at[mine], y_all.at[mine], dx_send.at[mine], y_recv.at[mine], 1, 0), go)

    def line_send(k, go):
        t = k * owners + mine

        @pl.when(owner & (p == k))
        def _():
            @pl.loop(0, rows - 1)
            def _(i):
                @pl.when((q != k) | (at_line(i) < k))
                def _():
                    act(remote(y_all.at[t], y_all.at[t], ln_send.at[i], y_recv.at[t], at_line(i), q), go)

    def has_whole(k, row, col):
        return ((row > k) & (col == k)) | ((row == k) & (col == k - 1))

    def has_made(k, row, col):
        return (row == k) & ((k == 0) | (col == k - 1))

    def plane_send(k, go):
        t = k * owners + mine

        @pl.when(owner)
        def _():
            @pl.loop(0, cols - 1)
            def _(i):
                d = at_plane(i)

                @pl.when(jnp.logical_not(has_whole(k, p, d)))
                def _():
                    act(remote(y_all.at[t], y_all.at[t], ag_send.at[k, i], y_recv.at[t], p, d), go)

    def solved_send(k, c, go):
        t = k * owners + c
        @pl.when(k < rows - 1)
        def _():
            act(remote(y_all.at[t], y_all.at[t], dx_send.at[c], y_recv.at[t], p + 1, k), go)

        @pl.when(c != q)
        def _():
            act(remote(y_all.at[t], y_all.at[t], sc_send.at[c], y_recv.at[t], p, c), go)

    def chain_send(k, c, go):
        t = k * owners + c

        @pl.when(p < rows - 1)
        def _():
            act(remote(y_all.at[t], y_all.at[t], ch_send.at[c], y_recv.at[t], p + 1, q), go)

    def v_send_one(j, c, go):
        act(remote(vout.at[c], vbuf.at[j, c], v_send.at[c], v_recv.at[j, c], p, p - 1), go)

    def y_wait(t):
        remote(y_all.at[t], y_all.at[t], ln_send.at[0], y_recv.at[t], p, at_plane(0)).wait_recv()

    def rhs_plane(go, when=True):
        @pl.when(owner & when)
        def _():
            @pl.loop(0, rows - 1)
            def _(j):
                t = at_line(j) * owners + mine
                if go:
                    remote(rhs_all.at[t], rhs_all.at[t], rl_send.at[0], r_recv.at[t], p, at_plane(0)).wait_recv()

                @pl.loop(0, cols - 1)
                def _(i):
                    act(remote(rhs_all.at[t], rhs_all.at[t], ra_send.at[j, i], r_recv.at[t], p, at_plane(i)), go)

    @pl.when(owner)
    def _():
        @pl.loop(0, cols - 1)
        def _(i):
            s = at_plane(i)
            remote(outp.at[mine], rs_buf.at[s], rs_send.at[mine], rs_recv.at[s], p, s).wait_recv()

        total = outp[mine]
        for i in range(cols - 1):
            total = total + rs_buf[at_plane(i)]

        @pl.when(p == 0)
        def _():
            y_all[mine] = -total

        @pl.when(solver)
        def _():
            ubuf[mine] = -total

        @pl.when((p > 0) & jnp.logical_not(solver))
        def _():
            usend[...] = -total

    first_send(True)
    df_send_one(True)

    rhs_plane(True, p >= 2)

    @pl.when(solver)
    def _():
        for c in range(owners):
            @pl.when(c != q)
            def _():
                remote(usend, ubuf.at[c], df_send, df_recv.at[c], p, at_plane(0)).wait_recv()

    @pl.loop(0, rows)
    def _(k):
        base = k * owners
        handed = (p > k) & (q == k)
        made = has_made(k, p, q)

        @pl.when(handed)
        def _():
            def take(i):
                for n in range(pair):
                    c = i * pair + n
                    y_wait(base + c)
                    chain_send(k, c, True)
                    xx[piece(c, tile), :] = turned(y_all[base + c])

            acc[...] = jnp.zeros_like(acc)

            @pl.loop(0, blocks - 1)
            def _(i):
                take(i)
                at = piece(i, step)
                weights = xx[at, :]
                acc[...] += nn(mhi[:, at], weights) + nn(mlo[:, at], weights)

            take(blocks - 1)
            last = order - step

            @pl.when(p == k + 1)
            def _():
                @pl.loop(0, k)
                def _(j):
                    @pl.loop(0, owners)
                    def _(c):
                        remote(vout.at[c], vbuf.at[j, c], v_send.at[c], v_recv.at[j, c], p, at_plane(0)).wait_recv()
                        ubuf[c] = ubuf[c] - vbuf[j, c]

            @pl.loop(0, blocks)
            def _(i):
                at = piece(i, step)
                weights = xx[last:, :]
                whole = acc[at, :] + nn(mhi[at, last:], weights) + nn(mlo[at, last:], weights)
                for n in range(pair):
                    c = i * pair + n
                    value = fold(whole[n * tile:(n + 1) * tile])

                    @pl.when(p == k + 1)
                    def _():
                        y_all[base + owners + c] = ubuf[c] - value
                        solved_send(k + 1, c, True)

                    @pl.when(p > k + 1)
                    def _():
                        vout[c] = value
                        v_send_one(k, c, True)

        @pl.when(owner & jnp.logical_not(made | handed))
        def _():
            y_wait(base + mine)

        line_send(k, True)

        plane_send(k, True)

        rhs_plane(True, (p == k) & (p < 2))

    load_force.wait()
    for t in range(tpd):
        @pl.loop(0, nnb)
        def _(n):
            high, low = halves(force[t, n])
            fhi[t, :, piece(n, tile)] = high
            flo[t, :, piece(n, tile)] = low

    @pl.loop(0, rows)
    def _(k):
        @pl.when(jnp.logical_not(has_whole(k, p, q)))
        def _():
            @pl.loop(0, cols - 1)
            def _(i):
                c = at_plane(i)

                @pl.when(c < owners)
                def _():
                    y_wait(k * owners + c)

    for c in range(owners):
        sol_out[:, c * tile:(c + 1) * tile] = y_all[p * owners + c]

    load_tlist.wait()
    load_nlist.wait()

    @pl.loop(0, rows - 1)
    def _(j):
        @pl.loop(0, cols - 1)
        def _(i):
            c = at_plane(i)

            @pl.when(c < owners)
            def _():
                t = at_line(j) * owners + c
                remote(rhs_all.at[t], rhs_all.at[t], rl_send.at[0], r_recv.at[t], p, at_plane(0)).wait_recv()

    for t in range(tpd):
        weights = jnp.concatenate([turned(y_all[nlist[0, t, n]]) for n in range(nnb)], axis=0)
        term = fold(nn(fhi[t], weights) + nn(flo[t], weights))
        res_out[0, t] = rhs_all[tlist[0, t]] - term

    rhs_line(False)

    @pl.loop(0, owners)
    def _(c):
        @pl.when(c != q)
        def _():
            rs_copy(c).wait_send()

    first_send(False)
    df_send_one(False)
    rhs_plane(False)
    @pl.loop(0, rows)
    def _(k):
        line_send(k, False)

        @pl.when((p == k) & (q == k - 1))
        def _():
            @pl.loop(0, owners)
            def _(c):
                solved_send(k, c, False)

        @pl.when((p > k) & (q == k))
        def _():
            @pl.loop(0, owners)
            def _(c):
                chain_send(k, c, False)

                @pl.when(p > k + 1)
                def _():
                    v_send_one(k, c, False)

        plane_send(k, False)


def per_device(rows, cols, window_rhs, past_solution, past_panel, window_panel, diag_inverse, tile_list, neighbor_list, force_constants):
    nrhs, order = window_rhs.shape
    depth = past_solution.shape[1]
    tpd, nnb, tile = force_constants.shape[1:4]
    owners = order // tile
    tiles = rows * owners
    hbm = pl.BlockSpec(memory_space=pltpu.HBM)
    vmem = pl.BlockSpec(memory_space=pltpu.VMEM)
    dma = pltpu.SemaphoreType.DMA
    return pl.pallas_call(
        functools.partial(kernel, rows, cols, owners, tile, nrhs, tpd, nnb),
        out_shape=(
            jax.ShapeDtypeStruct((nrhs, order), F32),
            jax.ShapeDtypeStruct((1, tpd, nrhs, tile), F32),
        ),
        in_specs=[hbm] * 8,
        out_specs=(vmem, vmem),
        scratch_shapes=[
            pltpu.SMEM((1, tpd), jnp.int32),
            pltpu.SMEM((1, tpd, nnb), jnp.int32),
            pltpu.VMEM((nrhs, depth), F32),
            pltpu.VMEM((order, depth), F32),
            pltpu.VMEM((order, order), F32),
            pltpu.VMEM((order, order), F32),
            pltpu.VMEM((tpd, nnb, tile, tile), F32),
            pltpu.VMEM((depth, 2 * nrhs), BF16),
            pltpu.VMEM((order, 2 * nrhs), BF16),
            pltpu.VMEM((order, order), BF16),
            pltpu.VMEM((order, order), BF16),
            pltpu.VMEM((order, order), BF16),
            pltpu.VMEM((order, order), BF16),
            pltpu.VMEM((tpd, tile, nnb * tile), BF16),
            pltpu.VMEM((tpd, tile, nnb * tile), BF16),
            pltpu.VMEM((order, 2 * nrhs), F32),
            pltpu.VMEM((owners, nrhs, tile), F32),
            pltpu.VMEM((cols, nrhs, tile), F32),
            pltpu.VMEM((owners, nrhs, tile), F32),
            pltpu.VMEM((nrhs, tile), F32),
            pltpu.VMEM((owners, nrhs, tile), F32),
            pltpu.VMEM((owners, nrhs, tile), F32),
            pltpu.VMEM((max(rows - 2, 1), owners, nrhs, tile), F32),
            pltpu.VMEM((tiles, nrhs, tile), F32),
            pltpu.VMEM((tiles, nrhs, tile), F32),
            dma((6,)),
            dma((owners,)),
            dma((owners,)),
            dma((owners,)),
            dma((cols,)),
            dma,
            dma((owners,)),
            dma((owners,)),
            dma((owners,)),
            dma((owners,)),
            dma((rows,)),
            dma((rows, cols)),
            dma((tiles,)),
            dma((rows,)),
            dma((rows, cols)),
            dma((tiles,)),
            dma((owners,)),
            dma((rows, owners)),
        ],
        compiler_params=pltpu.CompilerParams(
            collective_id=0, has_side_effects=True, vmem_limit_bytes=63 * 2**20
        ),
    )(window_rhs, past_solution, past_panel, window_panel, diag_inverse, tile_list, neighbor_list, force_constants)


def solution(mesh):
    placed = (
        P(None, "prow"),
        P(None, "pcol"),
        P("prow", "pcol"),
        P("prow", None, "pcol", None),
        P("prow", None, None),
        P(("prow", "pcol"), None),
        P(("prow", "pcol"), None, None),
        P(("prow", "pcol"), None, None, None, None),
    )
    return jax.shard_map(
        functools.partial(per_device, mesh.shape["prow"], mesh.shape["pcol"]),
        mesh=mesh,
        in_specs=placed,
        out_specs=(P(None, "prow"), P(("prow", "pcol"), None, None, None)),
        check_vma=False,
    )
```

```python
import functools

import jax
import jax.numpy as jnp
from jax import lax
from jax.experimental import pallas as pl
from jax.experimental.pallas import tpu as pltpu
from jax.sharding import PartitionSpec as P

MESH = pl.DeviceIdType.MESH
BF16 = jnp.bfloat16
F32 = jnp.float32


def halves(value):
    high = value.astype(BF16)
    return high, (value - high.astype(F32)).astype(BF16)


def nn(left, right):
    return lax.dot_general(left, right, (((1,), (0,)), ((), ())), preferred_element_type=F32)


def turned(block):
    high = block.astype(BF16).astype(F32)
    return jnp.concatenate([high, block - high], axis=0).T.astype(BF16)


def kernel(
    rows, cols, owners, tile, nrhs, tpd, nnb,
    rhs_hbm, psol_hbm, panel_hbm, win_hbm, dinv_hbm, tlist_hbm, nlist_hbm, force_hbm,
    sol_out, res_out,
    tlist, nlist, psol, panel, win, dinv, force, xpast, xx, whi, wlo, mhi, mlo, fhi, flo, acc,
    part, rs_buf, outp, usend, ubuf, vout, vbuf, y_all, rhs_all,
    out_sem, load_sem, panel_sem, rhs_sem,
    rs_send, rs_recv, df_send, df_recv, dx_send, ch_send, sc_send, ln_send, ag_send, y_recv,
    rl_send, ra_send, r_recv, v_send, v_recv,
):
    p = lax.axis_index("prow")
    q = lax.axis_index("pcol")
    order = owners * tile
    owner = q < owners
    mine = lax.rem(q, owners)
    barrier = pltpu.get_barrier_semaphore()

    def at_plane(step):
        return lax.rem(q + 1 + step, cols)

    def at_line(step):
        return lax.rem(p + 1 + step, rows)

    def remote(src, dst, send, recv, row, col):
        return pltpu.make_async_remote_copy(
            src_ref=src, dst_ref=dst, send_sem=send, recv_sem=recv,
            device_id=(row, col), device_id_type=MESH,
        )

    def act(copy, go):
        if go:
            copy.start()
        else:
            copy.wait_send()

    first = pltpu.make_async_copy(psol_hbm, psol, load_sem.at[0])
    first.start()

    def panel_copy(c):
        at = pl.ds(pl.multiple_of(c * tile, tile), tile)
        return pltpu.make_async_copy(panel_hbm.at[at, :], panel.at[at, :], panel_sem.at[c])

    @pl.loop(0, owners)
    def _(i):
        panel_copy(i).start()

    def rhs_copy(c):
        return pltpu.make_async_copy(
            rhs_hbm.at[:, c * tile:(c + 1) * tile], rhs_all.at[p * owners + c], rhs_sem.at[c]
        )

    for c in range(owners):
        rhs_copy(c).start()
    load_dinv = pltpu.make_async_copy(dinv_hbm.at[0], dinv, load_sem.at[1])
    load_win = pltpu.make_async_copy(win_hbm.at[0, :, 0, :], win, load_sem.at[2])
    load_force = pltpu.make_async_copy(force_hbm.at[0], force, load_sem.at[3])
    load_tlist = pltpu.make_async_copy(tlist_hbm, tlist, load_sem.at[4])
    load_nlist = pltpu.make_async_copy(nlist_hbm, nlist, load_sem.at[5])

    @pl.when(q < p)
    def _():
        load_win.start()

    load_tlist.start()
    load_nlist.start()

    @pl.loop(0, cols - 1)
    def _(i):
        pl.semaphore_signal(barrier, inc=1, device_id=(p, at_plane(i)), device_id_type=MESH)

    @pl.loop(0, rows - 1)
    def _(i):
        pl.semaphore_signal(barrier, inc=1, device_id=(at_line(i), q), device_id_type=MESH)

    @pl.when((p >= 2) & (q == p - 1))
    def _():
        pl.semaphore_signal(barrier, inc=1, device_id=(p - 1, q - 1), device_id_type=MESH)

    @pl.when((p == 1) & (q == 0))
    def _():
        @pl.loop(1, owners)
        def _(c):
            pl.semaphore_signal(barrier, inc=1, device_id=(0, c), device_id_type=MESH)

    first.wait()
    for at in range(0, psol.shape[1], tile):
        xpast[at:at + tile, :] = turned(psol[:, at:at + tile])

    def rhs_line(go):
        t = p * owners + mine

        @pl.when(owner)
        def _():
            @pl.loop(0, rows - 1)
            def _(i):
                act(remote(rhs_all.at[t], rhs_all.at[t], rl_send.at[i], r_recv.at[t], at_line(i), q), go)

    def fold(value):
        turned = value.T
        return turned[:nrhs] + turned[nrhs:]

    def pack(ref, base):
        for c in range(owners):
            xx[c * tile:(c + 1) * tile, :] = turned(ref[base + c])

    def rs_copy(c):
        return remote(outp.at[c], rs_buf.at[q], rs_send.at[c], rs_recv.at[q], p, c)

    step = min(256, order)
    pair = step // tile

    for i in range(order // step):
        for n in range(pair):
            panel_copy(i * pair + n).wait()

        if i == max(order // step // 2 - 1, 0):
            load_dinv.start()

        high, low = halves(panel[i * step:(i + 1) * step, :])
        weights = xpast[...]
        value = nn(high, weights) + nn(low, weights)
        for n in range(pair):
            part[i * pair + n] = fold(value[n * tile:(n + 1) * tile])

    load_force.start()
    for c in range(owners):
        rhs_copy(c).wait()
    passes_on = ((p == 0) & owner & (q > 0)) | ((p > 0) & (p < rows - 1) & (q == p - 1))
    pl.semaphore_wait(barrier, cols - 1 + rows - 1 + jnp.where(passes_on, 1, 0))

    rhs_line(True)

    @pl.when(q == 0)
    def _():
        for c in range(owners):
            part[c] = part[c] - rhs_all[p * owners + c]

    load_dinv.wait()
    pack(part, 0)
    for at in range(0, order, step):
        depth = at + step
        high, low = halves(dinv[at:depth, :depth])
        weights = xx[:depth, :]
        value = nn(high, weights) + nn(low, weights)
        for n in range(pair):
            c = at // tile + n
            outp[c] = fold(value[n * tile:(n + 1) * tile])

            @pl.when(c != q)
            def _():
                rs_copy(c).start()

    @pl.when(q < p)
    def _():
        load_win.wait()
        for at in range(0, order, step):
            high, low = halves(win[at:at + step, :])
            whi[at:at + step, :] = high
            wlo[at:at + step, :] = low
        for at in range(0, order, step):
            depth = at + step
            high, low = halves(dinv[at:at + step, :depth])
            value = nn(high, whi[:depth, :]) + nn(low, whi[:depth, :]) + nn(high, wlo[:depth, :])
            high, low = halves(value)
            mhi[at:at + step, :] = high
            mlo[at:at + step, :] = low

    solver = (p > 0) & (q == p - 1)

    def df_send_one(go):
        @pl.when(owner & (p > 0) & jnp.logical_not(solver))
        def _():
            act(remote(usend, ubuf.at[mine], df_send, df_recv.at[mine], p, p - 1), go)

    def first_send(go):
        @pl.when(owner & (p == 0))
        def _():
            act(remote(y_all.at[mine], y_all.at[mine], dx_send.at[mine], y_recv.at[mine], 1, 0), go)

    def line_send(k, go):
        t = k * owners + mine

        @pl.when(owner)
        def _():
            @pl.loop(0, rows - 1)
            def _(i):
                @pl.when((q != k) | (at_line(i) < k))
                def _():
                    act(remote(y_all.at[t], y_all.at[t], ln_send.at[i], y_recv.at[t], at_line(i), q), go)

    def has_whole(k, row, col):
        handed = (row > k) & (col == k)
        return handed if k == 0 else handed | ((row == k) & (col == k - 1))

    def plane_send(k, go):
        t = k * owners + mine

        @pl.when(owner)
        def _():
            @pl.loop(0, cols - 1)
            def _(i):
                d = at_plane(i)

                @pl.when(jnp.logical_not(has_whole(k, p, d)))
                def _():
                    act(remote(y_all.at[t], y_all.at[t], ag_send.at[k, i], y_recv.at[t], p, d), go)

    def solved_send(k, c, go):
        t = k * owners + c
        if k < rows - 1:
            act(remote(y_all.at[t], y_all.at[t], dx_send.at[c], y_recv.at[t], p + 1, k), go)

        @pl.when(c != q)
        def _():
            act(remote(y_all.at[t], y_all.at[t], sc_send.at[c], y_recv.at[t], p, c), go)

    def chain_send(k, c, go):
        t = k * owners + c

        @pl.when(p < rows - 1)
        def _():
            act(remote(y_all.at[t], y_all.at[t], ch_send.at[c], y_recv.at[t], p + 1, q), go)

    def v_send_one(j, c, go):
        act(remote(vout.at[c], vbuf.at[j, c], v_send.at[c], v_recv.at[j, c], p, p - 1), go)

    def y_wait(t):
        remote(y_all.at[t], y_all.at[t], ln_send.at[0], y_recv.at[t], p, at_plane(0)).wait_recv()

    def rhs_plane(go):
        @pl.when(owner)
        def _():
            @pl.loop(0, rows - 1)
            def _(j):
                t = at_line(j) * owners + mine
                if go:
                    remote(rhs_all.at[t], rhs_all.at[t], rl_send.at[0], r_recv.at[t], p, at_plane(0)).wait_recv()

                @pl.loop(0, cols - 1)
                def _(i):
                    act(remote(rhs_all.at[t], rhs_all.at[t], ra_send.at[j, i], r_recv.at[t], p, at_plane(i)), go)

    @pl.when(owner)
    def _():
        @pl.loop(0, cols - 1)
        def _(i):
            s = at_plane(i)
            remote(outp.at[mine], rs_buf.at[s], rs_send.at[mine], rs_recv.at[s], p, s).wait_recv()

        total = outp[mine]
        for i in range(cols - 1):
            total = total + rs_buf[at_plane(i)]

        @pl.when(p == 0)
        def _():
            y_all[mine] = -total

        @pl.when(solver)
        def _():
            ubuf[mine] = -total

        @pl.when((p > 0) & jnp.logical_not(solver))
        def _():
            usend[...] = -total

    first_send(True)
    df_send_one(True)

    @pl.when(p >= 2)
    def _():
        rhs_plane(True)

    @pl.when(solver)
    def _():
        for c in range(owners):
            @pl.when(c != q)
            def _():
                remote(usend, ubuf.at[c], df_send, df_recv.at[c], p, at_plane(0)).wait_recv()

    for k in range(rows):
        base = k * owners
        handed = (p > k) & (q == k)
        made = p == k if k == 0 else (p == k) & (q == k - 1)

        @pl.when(handed)
        def _():
            last = order - step
            for at in range(0, order, step):
                for n in range(pair):
                    c = at // tile + n
                    y_wait(base + c)
                    chain_send(k, c, True)
                    xx[c * tile:(c + 1) * tile, :] = turned(y_all[base + c])
                if at < last:
                    weights = xx[at:at + step, :]
                    value = nn(mhi[:, at:at + step], weights) + nn(mlo[:, at:at + step], weights)
                    acc[...] = value if at == 0 else acc[...] + value

            def product(at):
                weights = xx[last:, :]
                value = nn(mhi[at:at + step, last:], weights) + nn(mlo[at:at + step, last:], weights)
                return acc[at:at + step, :] + value

            @pl.when(p == k + 1)
            def _():
                for j in range(k):
                    @pl.loop(0, owners)
                    def _(c):
                        remote(vout.at[c], vbuf.at[j, c], v_send.at[c], v_recv.at[j, c], p, at_plane(0)).wait_recv()

                for at in range(0, order, step):
                    whole = product(at)
                    for n in range(pair):
                        c = at // tile + n
                        value = ubuf[c] - fold(whole[n * tile:(n + 1) * tile])
                        for j in range(k):
                            value = value - vbuf[j, c]
                        y_all[base + owners + c] = value
                        if k < rows - 1:
                            solved_send(k + 1, c, True)

            @pl.when(p > k + 1)
            def _():
                for at in range(0, order, step):
                    whole = product(at)
                    for n in range(pair):
                        c = at // tile + n
                        vout[c] = fold(whole[n * tile:(n + 1) * tile])
                        v_send_one(k, c, True)

        @pl.when(owner & jnp.logical_not(made | handed))
        def _():
            y_wait(base + mine)

        @pl.when(p == k)
        def _():
            line_send(k, True)

        plane_send(k, True)

        @pl.when((p == k) & (p < 2))
        def _():
            rhs_plane(True)

    load_force.wait()
    for t in range(tpd):
        for n in range(nnb):
            high, low = halves(force[t, n])
            fhi[t, :, n * tile:(n + 1) * tile] = high
            flo[t, :, n * tile:(n + 1) * tile] = low

    for k in range(rows):
        @pl.when(jnp.logical_not(has_whole(k, p, q)))
        def _():
            @pl.loop(0, cols - 1)
            def _(i):
                c = at_plane(i)

                @pl.when(c < owners)
                def _():
                    y_wait(k * owners + c)

    def sol_copy(c):
        return pltpu.make_async_copy(
            y_all.at[p * owners + c], sol_out.at[:, c * tile:(c + 1) * tile], out_sem.at[c]
        )

    for c in range(owners):
        sol_copy(c).start()

    load_tlist.wait()
    load_nlist.wait()

    @pl.loop(0, rows - 1)
    def _(j):
        @pl.loop(0, cols - 1)
        def _(i):
            c = at_plane(i)

            @pl.when(c < owners)
            def _():
                t = at_line(j) * owners + c
                remote(rhs_all.at[t], rhs_all.at[t], rl_send.at[0], r_recv.at[t], p, at_plane(0)).wait_recv()

    for t in range(tpd):
        weights = jnp.concatenate([turned(y_all[nlist[0, t, n]]) for n in range(nnb)], axis=0)
        term = fold(nn(fhi[t], weights) + nn(flo[t], weights))
        res_out[0, t] = rhs_all[tlist[0, t]] - term

    for c in range(owners):
        sol_copy(c).wait()

    rhs_line(False)

    @pl.loop(0, owners)
    def _(c):
        @pl.when(c != q)
        def _():
            rs_copy(c).wait_send()

    first_send(False)
    df_send_one(False)
    rhs_plane(False)
    for k in range(rows):
        @pl.when(p == k)
        def _():
            line_send(k, False)

        if k > 0:
            @pl.when((p == k) & (q == k - 1))
            def _():
                @pl.loop(0, owners)
                def _(c):
                    solved_send(k, c, False)

        @pl.when((p > k) & (q == k))
        def _():
            @pl.loop(0, owners)
            def _(c):
                chain_send(k, c, False)

                @pl.when(p > k + 1)
                def _():
                    v_send_one(k, c, False)

        plane_send(k, False)


def per_device(rows, cols, window_rhs, past_solution, past_panel, window_panel, diag_inverse, tile_list, neighbor_list, force_constants):
    nrhs, order = window_rhs.shape
    depth = past_solution.shape[1]
    tpd, nnb, tile = force_constants.shape[1:4]
    owners = order // tile
    tiles = rows * owners
    hbm = pl.BlockSpec(memory_space=pltpu.HBM)
    vmem = pl.BlockSpec(memory_space=pltpu.VMEM)
    dma = pltpu.SemaphoreType.DMA
    return pl.pallas_call(
        functools.partial(kernel, rows, cols, owners, tile, nrhs, tpd, nnb),
        out_shape=(
            jax.ShapeDtypeStruct((nrhs, order), F32),
            jax.ShapeDtypeStruct((1, tpd, nrhs, tile), F32),
        ),
        in_specs=[hbm] * 8,
        out_specs=(hbm, vmem),
        scratch_shapes=[
            pltpu.SMEM((1, tpd), jnp.int32),
            pltpu.SMEM((1, tpd, nnb), jnp.int32),
            pltpu.VMEM((nrhs, depth), F32),
            pltpu.VMEM((order, depth), F32),
            pltpu.VMEM((order, order), F32),
            pltpu.VMEM((order, order), F32),
            pltpu.VMEM((tpd, nnb, tile, tile), F32),
            pltpu.VMEM((depth, 2 * nrhs), BF16),
            pltpu.VMEM((order, 2 * nrhs), BF16),
            pltpu.VMEM((order, order), BF16),
            pltpu.VMEM((order, order), BF16),
            pltpu.VMEM((order, order), BF16),
            pltpu.VMEM((order, order), BF16),
            pltpu.VMEM((tpd, tile, nnb * tile), BF16),
            pltpu.VMEM((tpd, tile, nnb * tile), BF16),
            pltpu.VMEM((order, 2 * nrhs), F32),
            pltpu.VMEM((owners, nrhs, tile), F32),
            pltpu.VMEM((cols, nrhs, tile), F32),
            pltpu.VMEM((owners, nrhs, tile), F32),
            pltpu.VMEM((nrhs, tile), F32),
            pltpu.VMEM((owners, nrhs, tile), F32),
            pltpu.VMEM((owners, nrhs, tile), F32),
            pltpu.VMEM((max(rows - 2, 1), owners, nrhs, tile), F32),
            pltpu.VMEM((tiles, nrhs, tile), F32),
            pltpu.VMEM((tiles, nrhs, tile), F32),
            dma((owners,)),
            dma((6,)),
            dma((owners,)),
            dma((owners,)),
            dma((owners,)),
            dma((cols,)),
            dma,
            dma((owners,)),
            dma((owners,)),
            dma((owners,)),
            dma((owners,)),
            dma((rows,)),
            dma((rows, cols)),
            dma((tiles,)),
            dma((rows,)),
            dma((rows, cols)),
            dma((tiles,)),
            dma((owners,)),
            dma((rows, owners)),
        ],
        compiler_params=pltpu.CompilerParams(
            collective_id=0, has_side_effects=True, vmem_limit_bytes=63 * 2**20
        ),
    )(window_rhs, past_solution, past_panel, window_panel, diag_inverse, tile_list, neighbor_list, force_constants)


def solution(mesh):
    placed = (
        P(None, "prow"),
        P(None, "pcol"),
        P("prow", "pcol"),
        P("prow", None, "pcol", None),
        P("prow", None, None),
        P(("prow", "pcol"), None),
        P(("prow", "pcol"), None, None),
        P(("prow", "pcol"), None, None, None, None),
    )
    return jax.shard_map(
        functools.partial(per_device, mesh.shape["prow"], mesh.shape["pcol"]),
        mesh=mesh,
        in_specs=placed,
        out_specs=(P(None, "prow"), P(("prow", "pcol"), None, None, None)),
        check_vma=False,
    )
```
